32 devices in a mesh: group: 2 (over y), tile: 4 (over z), sect: 2 (over x), sub: 2 (over core).
Axes of the slice: x: 2, y: 2, z: 4, core: 2. Of those that a mesh axis runs over, the one named last changes fastest.
Arguments:
- air_state: float32 [4, 80, 64, 256], P(None, ('sect', 'sub'), ('group', 'tile')), parts along dimension 2, may hold values from -3 to 3
- fire_level: float32 [640, 2560], P(('group', 'tile'), ('sect', 'sub')), parts along dimension 0, may hold values from 0.2 to 3
- fuel_left: float32 [640, 2560], P(('group', 'tile'), ('sect', 'sub')), parts along dimension 0, may hold values from 0.3 to 1
- fuel_class: int32 [640, 2560], P(('group', 'tile'), ('sect', 'sub')), parts along dimension 0, may hold values from 0 to 12
- ignition: int32 [640, 2560], P(('group', 'tile'), ('sect', 'sub')), parts along dimension 0, may hold values from 0 to 4, as said below
- plan: int32 [4], replicated, may hold values from 1 to 3
- spread_rate: float32 [13], replicated, may hold values from 0.05 to 0.3
- burn_time: float32 [13], replicated, may hold values from 0.5 to 8
- heat_content: float32 [13], replicated, may hold values from 1 to 10
- moisture_content: float32 [13], replicated, may hold values from 0.1 to 1
Outputs:
- air_out: float32 [4, 80, 64, 256], P(None, ('sect', 'sub'), ('group', 'tile')), parts along dimension 2
- level_out: float32 [640, 2560], P(('group', 'tile'), ('sect', 'sub')), parts along dimension 0
- fuel_out: float32 [640, 2560], P(('group', 'tile'), ('sect', 'sub')), parts along dimension 0
The draws below stay inside these ranges and needn't reach their ends.
There are 2 independent parts, one for each index of `group`. The reference program is written for one: setup_inputs(seed, part) draws one part's arguments, and reference() takes and returns one part's arrays. A program takes and returns all parts, laid end to end along the dimension named above; an argument that names none is the same for every part. Nothing has to cross between parts.
Inputs may be any that keep to these rules, and one draw needn't show every extreme that they name: `ignition`: A cell with value c is ignited at the start of coupling step c; cells with value 4 are not ignited in the window. Ignited cells lie in scattered atmosphere columns. The plan is shared by all scenarios.
All inputs are finite; a program needn't handle non-finite values.
Results may differ from the reference program's by a relative error of at most 0.0001.
Values sent between devices are 32-bit elements; how exact they have to be, the bound alone decides.
No kernel may reach another device: no remote copies, remote signals or barrier semaphores. Data moves between devices by JAX's collectives and lax.ppermute only.
A program may use at most 128 MiB of HBM per device.

```python
import math
import jax
import jax.numpy as jnp
import numpy as np
from jax import lax

LEVELS = 80
REFINE = 10
NFUEL = 13
STEPS = 4
SUBSTEPS = 4
NX = 32
NY = 256
FIRE_X = 320
FIRE_Y = 2560


def draw_ignition(key, part):
    first_key, second_key, third_key = jax.random.split(key, 3)
    active = jax.random.randint(first_key, (NX, NY), 0, 8) == 0
    ignite_at = jax.random.randint(second_key, (NX, NY), 0, STEPS)
    coarse_map = jnp.where(active, ignite_at, STEPS)
    fine_map = jnp.repeat(jnp.repeat(coarse_map, REFINE, axis=0), REFINE, axis=1)
    chosen = jax.random.randint(third_key, (FIRE_X, FIRE_Y), 0, 4) == 0
    return jnp.where(chosen, fine_map, STEPS).astype(jnp.int32)


def place_ends(values, rng, smallest, top_value):
    dims = values.shape
    place = [jax.random.randint(jax.random.fold_in(rng, axis), (), 0, dims[axis]) for axis in range(len(dims))]
    values = values.at[tuple(place)].set(smallest)
    longest = dims.index(max(dims))
    place[longest] = (place[longest] + 1) % dims[longest]
    return values.at[tuple(place)].set(top_value)


def levels(own_key, dims, shards, least, largest):
    def one(position, shards_of):
        steps = jax.random.uniform(jax.random.fold_in(jax.random.fold_in(own_key, 6), position), (shards_of,), jnp.float32, least / len(shards), largest / len(shards))
        return jnp.repeat(jnp.exp(steps), dims[position] // shards_of).reshape((-1,) + (1,) * (len(dims) - position - 1))

    loudness = one(*shards[0])
    for cut in shards[1:]:
        loudness = loudness * one(*cut)
    return loudness


def rank_table(count, lean):
    portions = [(1 << 20) // math.isqrt(grade ** lean) + 1 for grade in range(1, count + 1)]
    deviation = 1 + sum(portions) // (1 << 30)
    return np.cumsum(np.array([max(1, weight // deviation) for weight in portions]))


def ranked_ids(rng, dims, amount, lean):
    listing = rank_table(amount, lean)
    ticket = jax.random.randint(jax.random.fold_in(rng, 1), dims, 0, int(listing[amount - 1]))
    standing = jnp.searchsorted(jnp.asarray(listing, jnp.int32), ticket, side="right")
    return jax.random.permutation(jax.random.fold_in(rng, 2), amount)[standing].astype(jnp.int32)


def centred(own_key, extent, deviation, reach, cuts=(), dtype=jnp.bfloat16):
    drawn = deviation * jax.random.normal(own_key, extent, jnp.float32)
    if cuts:
        drawn = drawn * levels(own_key, extent, cuts, -0.22, 0.18)
    return jnp.clip(drawn, -reach, reach).astype(dtype)


def setup_inputs(seed: int = 0, part: int = 0) -> dict:
    arg_keys = jax.random.split(jax.random.key(seed), 11)
    own_keys = jax.random.split(jax.random.fold_in(arg_keys[10], part), 11)
    air_state = centred(own_keys[0], (4, LEVELS, NX, NY), 1.0, 3.0, ((1, 4), (2, 4)), jnp.float32)
    fire_level = jnp.clip(0.2 + 2.8 * jax.random.uniform(own_keys[1], (FIRE_X, FIRE_Y), jnp.float32) ** levels(own_keys[1], (FIRE_X, FIRE_Y), ((0, 4), (1, 4)), -0.2, 0.2), 0.2, 3.0)
    fuel_left = jnp.clip(0.3 + 0.7 * jax.random.uniform(own_keys[2], (FIRE_X, FIRE_Y), jnp.float32) ** levels(own_keys[2], (FIRE_X, FIRE_Y), ((0, 4), (1, 4)), -0.2, 0.2), 0.3, 1.0)
    fuel_class = place_ends(ranked_ids(own_keys[3], (FIRE_X, FIRE_Y), NFUEL, 2), jax.random.fold_in(own_keys[3], 3), 0, NFUEL - 1).astype(jnp.int32)
    ignition = draw_ignition(jax.random.fold_in(jax.random.fold_in(arg_keys[10], part), 71), part)
    plan = place_ends(jax.random.randint(arg_keys[5], (STEPS,), 1, 4), jax.random.fold_in(arg_keys[5], 1), 1, 3).astype(jnp.int32)
    spread_rate = jnp.clip(jnp.exp(jax.random.uniform(arg_keys[6], (NFUEL,), jnp.float32, math.log(0.05), math.log(0.3))), 0.05, 0.3)
    burn_time = jnp.clip(jnp.exp(jax.random.uniform(arg_keys[7], (NFUEL,), jnp.float32, math.log(0.5), math.log(8.0))), 0.5, 8.0)
    heat_content = jnp.clip(jnp.exp(jax.random.uniform(arg_keys[8], (NFUEL,), jnp.float32, math.log(1.0), math.log(10.0))), 1.0, 10.0)
    moisture_content = jnp.clip(jnp.exp(jax.random.uniform(arg_keys[9], (NFUEL,), jnp.float32, math.log(0.1), math.log(1.0))), 0.1, 1.0)
    return dict(air_state=air_state, fire_level=fire_level, fuel_left=fuel_left, fuel_class=fuel_class, ignition=ignition, plan=plan, spread_rate=spread_rate, burn_time=burn_time, heat_content=heat_content, moisture_content=moisture_content)


air_delta = 0.1
diffusion = 0.2
heat_gain = 20.0
vapour_gain = 20.0
lift_gain = 0.3
wind_gain = 0.5
fire_delta = 0.15

def level_weights(layer_count):
    height = jnp.arange(layer_count).astype(jnp.float32)
    profile = jnp.exp(-2.0 * height / layer_count)
    profile = layer_count * profile / jnp.sum(profile)
    column = jnp.exp(-height / layer_count)
    column = column / jnp.sum(column)
    return (profile, column)

def fire_core(padded, fuel_now, energy, vapour, rate_cell, burnout, heat_cell, moist_cell, wind_east, wind_north, fire_step):
    at_centre = padded[1:-1, 1:-1]
    at_west = padded[:-2, 1:-1]
    at_east = padded[2:, 1:-1]
    at_south = padded[1:-1, :-2]
    at_north = padded[1:-1, 2:]
    steepness = jnp.sqrt(jnp.maximum(at_centre - at_west, 0.0) ** 2 + jnp.minimum(at_east - at_centre, 0.0) ** 2 + jnp.maximum(at_centre - at_south, 0.0) ** 2 + jnp.minimum(at_north - at_centre, 0.0) ** 2)
    grad_east = 0.5 * (at_east - at_west)
    grad_north = 0.5 * (at_north - at_south)
    tailwind = (wind_east * grad_east + wind_north * grad_north) / jnp.sqrt(grad_east * grad_east + grad_north * grad_north + 1.0)
    fire_speed = rate_cell * (1.0 + wind_gain * jnp.maximum(tailwind, 0.0))
    level_set = at_centre - fire_step * fire_speed * steepness
    burning = jnp.clip(0.5 - level_set, 0.0, 1.0)
    remain = fuel_now * jnp.exp(-fire_step * burning / burnout)
    consumed = fuel_now - remain
    return (level_set, remain, energy + consumed * heat_cell, vapour + consumed * moist_cell)

def air_core(padded, flux_coarse, profile):
    at_centre = padded[:, 1:-1, 1:-1, 1:-1]
    at_below = padded[:, :-2, 1:-1, 1:-1]
    at_above = padded[:, 2:, 1:-1, 1:-1]
    at_west = padded[:, 1:-1, :-2, 1:-1]
    at_east = padded[:, 1:-1, 2:, 1:-1]
    at_south = padded[:, 1:-1, 1:-1, :-2]
    at_north = padded[:, 1:-1, 1:-1, 2:]
    speed_east = at_centre[2]
    speed_north = at_centre[3]
    advect = jnp.maximum(speed_east, 0.0) * (at_centre - at_west) + jnp.minimum(speed_east, 0.0) * (at_east - at_centre) + jnp.maximum(speed_north, 0.0) * (at_centre - at_south) + jnp.minimum(speed_north, 0.0) * (at_north - at_centre)
    diffused = at_west + at_east + at_south + at_north + at_below + at_above - 6.0 * at_centre
    lift_east = at_east[0] + 0.6 * at_east[1] - (at_west[0] + 0.6 * at_west[1])
    lift_north = at_north[0] + 0.6 * at_north[1] - (at_south[0] + 0.6 * at_south[1])
    heights = profile[:, None, None]
    forcing = jnp.stack([heat_gain * flux_coarse[0][None] * heights, vapour_gain * flux_coarse[1][None] * heights, 0.5 * lift_gain * lift_east, 0.5 * lift_gain * lift_north])
    return at_centre + air_delta * (diffusion * diffused - advect + forcing)

def coarsen(fine_field, refine_by):
    channels, row_count, col_count = fine_field.shape
    blocks = fine_field.reshape(channels, row_count // refine_by, refine_by, col_count // refine_by, refine_by)
    return lax.optimization_barrier(jnp.sum(blocks, axis=(2, 4))) / (refine_by * refine_by)

def reference(air_state, fire_level, fuel_left, fuel_class, ignition, plan, spread_rate, burn_time, heat_content, moisture_content):
    rate_cell = spread_rate[fuel_class]
    burnout = burn_time[fuel_class]
    heat_cell = heat_content[fuel_class]
    moist_cell = moisture_content[fuel_class]
    profile, column = level_weights(LEVELS)
    air_field = air_state
    level_set = fire_level
    fuel_now = fuel_left
    for coupling in range(STEPS):
        wind_coarse = lax.optimization_barrier(jnp.sum(column[None, :, None, None] * air_field[2:4], axis=1))
        wind_fine = jnp.repeat(jnp.repeat(wind_coarse, REFINE, axis=1), REFINE, axis=2)
        fire_step = plan[coupling].astype(jnp.float32) * fire_delta
        level_set = jnp.where(ignition <= coupling, jnp.minimum(level_set, -1.0), level_set)
        energy = jnp.zeros_like(level_set)
        vapour = jnp.zeros_like(level_set)
        for sub_step in range(SUBSTEPS):
            padded = jnp.pad(level_set, 1, mode='edge')
            level_set, fuel_now, energy, vapour = fire_core(padded, fuel_now, energy, vapour, rate_cell, burnout, heat_cell, moist_cell, wind_fine[0], wind_fine[1], fire_step)
        flux_coarse = coarsen(jnp.stack([energy, vapour]), REFINE)
        padded_air = jnp.pad(air_field, ((0, 0), (1, 1), (1, 1), (1, 1)))
        air_field = air_core(padded_air, flux_coarse, profile)
    return (air_field, level_set, fuel_now)
```

```python
import functools

import jax
import jax.numpy as jnp
import numpy as np
from jax import lax
from jax.experimental import pallas as pl
from jax.experimental.pallas import tpu as pltpu
from jax.sharding import PartitionSpec as P

LEVELS = 80
REFINE = 10
STEPS = 4
SUBSTEPS = 4
NFUEL = 13

LANES = 128
HALO = STEPS
EDGE = HALO * REFINE
PAD = 8

air_delta = 0.1
diffusion = 0.2
heat_gain = 20.0
vapour_gain = 20.0
lift_gain = 0.3
wind_gain = 0.5
fire_delta = 0.15

BANDS = ("sect", "sub")
VMEM_LIMIT = 48 * 1024 * 1024


def iota(shape, dim):
    return lax.broadcasted_iota(jnp.int32, shape, dim)


def roll(value, shift, axis):
    return pltpu.roll(value, shift, axis)


def level_weights(layer_count):
    height = np.arange(layer_count).astype(np.float64)
    profile = np.exp(-2.0 * height / layer_count)
    profile = layer_count * profile / np.sum(profile)
    column = np.exp(-height / layer_count)
    column = column / np.sum(column)
    return profile.astype(np.float32), column.astype(np.float32)


def air_tiles(depth):
    return 2 * depth + -(-depth // 3)


def pack_kernel(bands, at_ref, air_ref, level_ref, fuel_ref, class_ref, ignite_ref, *outs):
    slots, up_ref, down_ref = outs[:bands], outs[bands], outs[bands + 1]
    depth = air_ref.shape[1]
    lane_tiles = air_ref.shape[3] // LANES
    rows, width = level_ref.shape
    lane = iota((8, LANES), 1)
    fields = [ref[...] for ref in (level_ref, fuel_ref)]
    fields += [ref[...].astype(jnp.float32) for ref in (class_ref, ignite_ref)]
    for a, field in enumerate(fields):
        for j in range(width // LANES):
            cols = field[:, j * LANES : (j + 1) * LANES]
            up_ref[a, j] = cols[:EDGE]
            down_ref[a, j] = cols[rows - EDGE :]
    base = air_tiles(depth)
    wide = iota((rows, LANES), 1)
    for pair in range(2):
        first, second = fields[2 * pair], fields[2 * pair + 1]
        at = pl.ds(base + pair * (rows // 8), rows // 8)
        to_next = jnp.where(wide < 64, roll(second[:, width - LANES :], 64, 1), first[:, width - LANES :])
        slots[1][at] = to_next.reshape(rows // 8, 8, LANES)
        to_prev = jnp.where(wide < 64, first[:, :LANES], roll(second[:, :LANES], 64, 1))
        slots[bands - 1][at] = to_prev.reshape(rows // 8, 8, LANES)
    band = at_ref[1]
    for k in range(bands):
        dest = lax.rem(band + k, bands)
        odd = lax.rem(dest, 2)
        own = pl.multiple_of((dest // 2) * LANES, LANES)
        high = (dest + 1) // 2
        right = pl.multiple_of(jnp.minimum(high, lane_tiles - 1) * LANES, LANES)
        left = pl.multiple_of(jnp.maximum(high - 1, 0) * LANES, LANES)
        turn = 64 * odd
        back = 64 - turn
        from_right = lane < 96 - turn
        for l in range(depth):
            for p in range(2):
                first = air_ref[2 * p, l, :, pl.ds(own, LANES)]
                second = air_ref[2 * p + 1, l, :, pl.ds(own, LANES)]
                slots[k][2 * l + p] = jnp.where(lane < 64, roll(first, turn, 1), roll(second, back, 1))
        for g in range(-(-depth // 3)):
            packed = jnp.zeros((8, LANES), jnp.float32)
            for l in range(3 * g, min(3 * g + 3, depth)):
                for f in range(4):
                    j = (l - 3 * g) * 4 + f
                    edge = jnp.where(
                        from_right, air_ref[f, l, :, pl.ds(right, LANES)], air_ref[f, l, :, pl.ds(left, LANES)]
                    )
                    edge = roll(edge, 4 * j + back, 1)
                    here = ((lane >= 4 * j) & (lane < 4 * j + 4)) | ((lane >= 60 + 4 * j) & (lane < 64 + 4 * j))
                    packed = jnp.where(here, edge, packed)
            slots[k][2 * depth + g] = packed


def corner_tiles(next_ref, prev_ref, base, rows):
    lane = iota((rows, LANES), 1)
    result = []
    for pair in range(2):
        at = pl.ds(base + pair * (rows // 8), rows // 8)
        left = prev_ref[at].reshape(rows, LANES)
        right = next_ref[at].reshape(rows, LANES)
        result.append(jnp.where(lane < 64, right, left))
        result.append(roll(jnp.where(lane < 64, left, right), 64, 1))
    return result


def relay_kernel(bands, rows, *refs):
    slots, up_ref, down_ref = refs[:bands], refs[bands], refs[bands + 1]
    tiles = slots[0].shape[0]
    sub = iota((8, LANES), 0)
    for half in range(bands // 2):
        one, two = slots[2 * half], slots[2 * half + 1]

        def body(i, carry, one=one, two=two, half=half):
            first, second = one[i], two[i]
            up_ref[half * tiles + i] = jnp.where(sub < 4, first, roll(second, 4, 0))
            down_ref[half * tiles + i] = jnp.where(sub < 4, roll(first, 4, 0), second)
            return carry

        lax.fori_loop(0, tiles, body, 0)
    corners = corner_tiles(slots[bands - 1], slots[1], tiles, rows)
    base = (bands // 2) * tiles
    count = EDGE // 8
    for a, corner in enumerate(corners):
        at = pl.ds(base + a * count, count)
        up_ref[at] = corner[:EDGE].reshape(count, 8, LANES)
        down_ref[at] = corner[rows - EDGE :].reshape(count, 8, LANES)


def main_kernel(
    bands,
    at_ref,
    plan_ref,
    tables_ref,
    weights_ref,
    level_in,
    fuel_in,
    class_in,
    ignite_in,
    *refs,
):
    slots = refs[:bands]
    fire_up, fire_down, edge_up, edge_down = refs[bands : bands + 4]
    level_out, fuel_out = refs[bands + 4 : bands + 6]
    outs = refs[bands + 6 : 2 * bands + 6]
    (lev_a, lev_b, fuel, ignite, rate, decay, heat, moist, burnt, wind_u, wind_v, energy, vapour, air_a, air_b) = refs[
        2 * bands + 6 :
    ]
    tile, band, tile_count = at_ref[0], at_ref[1], at_ref[2]
    rows, width = level_in.shape
    tiles = width // LANES
    depth = LEVELS // bands
    count = air_tiles(depth)
    own = PAD + EDGE
    span = rows + 2 * EDGE
    lane = iota((8, LANES), 1)

    corners = corner_tiles(slots[bands - 1], slots[1], count, rows)
    base = (bands // 2) * count
    for a, (source, scratch) in enumerate(
        ((level_in, lev_a), (fuel_in, fuel), (class_in, rate), (ignite_in, ignite))
    ):
        for j in range(tiles):
            scratch[j, PAD:own] = fire_up[a, j]
            scratch[j, own : own + rows] = source[:, j * LANES : (j + 1) * LANES].astype(jnp.float32)
            scratch[j, own + rows : own + rows + EDGE] = fire_down[a, j]
        at = pl.ds(base + a * (EDGE // 8), EDGE // 8)
        scratch[tiles, PAD:own] = edge_up[at].reshape(EDGE, LANES)
        scratch[tiles, own : own + rows] = corners[a]
        scratch[tiles, own + rows : own + rows + EDGE] = edge_down[at].reshape(EDGE, LANES)
    spare = jnp.zeros((tiles + 1, PAD, LANES), jnp.float32)
    for scratch in (lev_a, lev_b):
        scratch[:, :PAD] = spare
        scratch[:, PAD + span :] = spare
    for scratch in (energy, vapour):
        scratch[...] = jnp.zeros_like(scratch)

    vectors = []
    for n in range(4):
        vector = jnp.zeros((8, LANES), jnp.float32)
        for category in range(NFUEL):
            vector = jnp.where(lane == category, tables_ref[n, category], vector)
        vectors.append(vector)
    vectors[1] = -1.0 / jnp.where(lane < NFUEL, vectors[1], 1.0)

    def lookup(t, carry):
        at = pl.ds(pl.multiple_of(PAD + 8 * t, 8), 8)
        for j in range(tiles + 1):
            index = rate[j, at].astype(jnp.int32)
            for vector, scratch in zip(vectors, (rate, decay, heat, moist)):
                scratch[j, at] = jnp.take_along_axis(vector, index, axis=1, mode="promise_in_bounds")
        return carry

    lax.fori_loop(0, span // 8, lookup, 0)

    row16 = iota((16, LANES), 0)
    lane16 = iota((16, LANES), 1)
    first_tile, final_tile = tile == 0, tile == tile_count - 1
    first_band, final_band = band == 0, band == bands - 1
    low_row = jnp.where(final_tile, 8, 12)
    high_row = jnp.where(first_tile, 16, 12)
    low_lane = jnp.where(final_band, 64, 68)
    high_lane = jnp.where(first_band, 128, 124)
    inside = ((row16 < low_row) | (row16 >= high_row)) & ((lane16 < low_lane) | (lane16 >= high_lane))
    sub = iota((8, LANES), 0)
    for k in range(bands):
        source = lax.rem(band - k + bands, bands)
        half = k // 2

        def whole(i, k=k, half=half):
            below, above = edge_down[half * count + i], edge_up[half * count + i]
            if k % 2 == 0:
                halo = jnp.where(sub < 4, below, roll(above, 4, 0))
            else:
                halo = jnp.where(sub < 4, roll(below, 4, 0), above)
            return jnp.concatenate([slots[k][i], halo], axis=0)

        for g in range(-(-depth // 3)):
            edges = whole(2 * depth + g)
            for l in range(3 * g, min(3 * g + 3, depth)):
                level_at = source * depth + l + 1
                for p in range(2):
                    both = whole(2 * l + p)
                    for f in range(2):
                        j = (l - 3 * g) * 4 + 2 * p + f
                        inner = both if f == 0 else roll(both, 64, 1)
                        value = jnp.where(lane16 < 64, inner, roll(edges, 64 - 4 * j, 1))
                        air_a[2 * p + f, level_at] = jnp.where(inside, value, 0.0)
    nothing = jnp.zeros((16, LANES), jnp.float32)
    for scratch in (air_a, air_b):
        for f in range(4):
            scratch[f, 0] = nothing
            scratch[f, LEVELS + 1] = nothing

    cell, column = iota((LANES, LANES), 0), iota((LANES, LANES), 1)
    start = jnp.where(
        column < 64 + HALO,
        REFINE * column,
        jnp.where(column >= LANES - HALO, REFINE * column + (tiles + 1) * LANES - REFINE * LANES, -LANES * 1000),
    )
    across = []
    for j in range(tiles + 1):
        place = cell + j * LANES
        across.append(jnp.where((place >= start) & (place < start + REFINE), 1.0, 0.0).astype(jnp.float32))
    cell, column = iota((span, 16), 0), iota((span, 16), 1)
    start = jnp.where(column < 8 + HALO, EDGE + REFINE * column, REFINE * (column - 12))
    along = jnp.where((cell >= start) & (cell < start + REFINE), 1.0, 0.0).astype(jnp.float32)

    def dot(a, b, dims):
        return lax.dot_general(
            a, b, (dims, ((), ())), precision=lax.Precision.HIGHEST, preferred_element_type=jnp.float32
        )

    def first_wind(k, carry):
        weight = weights_ref[1, k]
        return (carry[0] + weight * air_a[2, k + 1], carry[1] + weight * air_a[3, k + 1])

    wind = lax.fori_loop(0, LEVELS, first_wind, (nothing, nothing))

    def mend_rows(scratch):
        @pl.when(first_tile)
        def _():
            for j in range(tiles + 1):
                scratch[j, own - 1 : own] = scratch[j, own : own + 1]

        @pl.when(final_tile)
        def _():
            for j in range(tiles + 1):
                scratch[j, own + rows : own + rows + 1] = scratch[j, own + rows - 1 : own + rows]

    mend_low = first_band & (lane == LANES - 1)
    mend_high = final_band & (lane == 0)

    def mend_lanes(values):
        halo = jnp.where(mend_low, roll(values[0], LANES - 1, 1), values[tiles])
        halo = jnp.where(mend_high, roll(values[tiles - 1], 1, 1), halo)
        return values[:tiles] + [halo]

    state, other = air_a, air_b
    for c in range(STEPS):
        reach = EDGE - REFINE * (c + 1)
        fire_step = plan_ref[c].astype(jnp.float32) * fire_delta
        wide = [dot(w * wind_gain, m, ((1,), (1,))) for w in wind for m in across]
        for j in range(tiles + 1):
            wind_u[j] = dot(along, wide[j], ((1,), (0,)))
            wind_v[j] = dot(along, wide[tiles + 1 + j], ((1,), (0,)))

        def strips(margin):
            return (EDGE - margin) // 8, -(-(EDGE + rows + margin) // 8)

        def kindle(t, carry, c=c):
            at = pl.ds(pl.multiple_of(PAD + 8 * t, 8), 8)
            values = []
            for j in range(tiles + 1):
                value = lev_a[j, at]
                values.append(jnp.where(ignite[j, at] <= c, jnp.minimum(value, -1.0), value))
            for j, value in enumerate(mend_lanes(values)):
                lev_a[j, at] = value
            return carry

        lax.fori_loop(*strips(reach + SUBSTEPS), kindle, 0)
        mend_rows(lev_a)
        before, after = lev_a, lev_b
        for s in range(SUBSTEPS):

            def advance(t, carry, s=s, before=before, after=after):
                row = pl.multiple_of(PAD + 8 * t, 8)
                at = pl.ds(row, 8)
                flat = pl.ds(pl.multiple_of(8 * t, 8), 8)
                centre = [before[j, at] for j in range(tiles + 1)]
                lower = [roll(value, 1, 1) for value in centre]
                upper = [roll(value, LANES - 1, 1) for value in centre]
                result = []
                for j in range(tiles + 1):
                    west = before[j, pl.ds(row - 1, 8)]
                    east = before[j, pl.ds(row + 1, 8)]
                    south = jnp.where(lane == 0, lower[j - 1], lower[j])
                    north = jnp.where(lane == LANES - 1, upper[(j + 1) % (tiles + 1)], upper[j])
                    here = centre[j]
                    back, ahead = here - west, east - here
                    below, above = here - south, north - here
                    a, b = jnp.maximum(back, 0.0), jnp.minimum(ahead, 0.0)
                    d, e = jnp.maximum(below, 0.0), jnp.minimum(above, 0.0)
                    square = (a * a + b * b) + (d * d + e * e)
                    steep = square * lax.rsqrt(jnp.maximum(square, 1.2e-38))
                    gx, gy = back + ahead, below + above
                    tail = (wind_u[j, flat] * gx + wind_v[j, flat] * gy) * lax.rsqrt((gx * gx + 4.0) + gy * gy)
                    speed = (fire_step * rate[j, at]) * (1.0 + jnp.maximum(tail, 0.0))
                    result.append(here - speed * steep)
                for j in range(tiles + 1):
                    burning = jnp.clip(0.5 - result[j], 0.0, 1.0)
                    if s > 0:
                        burning = burning + burnt[j, at]
                    if s < SUBSTEPS - 1:
                        burnt[j, at] = burning
                    else:
                        held = fuel[j, at]
                        remain = held * jnp.exp(burning * (fire_step * decay[j, at]))
                        spent = held - remain
                        fuel[j, at] = remain
                        energy[j, flat] = spent * heat[j, at]
                        vapour[j, flat] = spent * moist[j, at]
                for j, value in enumerate(mend_lanes(result)):
                    after[j, at] = value
                return carry

            lax.fori_loop(*strips(reach + SUBSTEPS - 1 - s), advance, 0)
            if s < SUBSTEPS - 1:
                mend_rows(after)
            before, after = after, before

        flux = []
        for scratch in (energy, vapour):
            total = dot(scratch[0], across[0], ((1,), (0,)))
            for j in range(1, tiles + 1):
                total = total + dot(scratch[j], across[j], ((1,), (0,)))
            flux.append(dot(along, total, ((0,), (0,))) * (1.0 / (REFINE * REFINE)))
        heat_in = flux[0] * (air_delta * heat_gain)
        vapour_in = flux[1] * (air_delta * vapour_gain)

        def air_step(k, state=state, heat_in=heat_in, vapour_in=vapour_in):
            here = [state[f, k + 1] for f in range(4)]
            u, v = here[2], here[3]
            spread = air_delta * diffusion
            to_west = spread + air_delta * jnp.maximum(u, 0.0)
            to_east = spread - air_delta * jnp.minimum(u, 0.0)
            to_south = spread + air_delta * jnp.maximum(v, 0.0)
            to_north = spread - air_delta * jnp.minimum(v, 0.0)
            keep = (1.0 - 2.0 * spread) - ((to_west + to_east) + (to_south + to_north))
            height = weights_ref[0, k]
            sides = []
            result = []
            for f in range(4):
                west, east = roll(here[f], 1, 0), roll(here[f], 15, 0)
                south, north = roll(here[f], 1, 1), roll(here[f], LANES - 1, 1)
                if f < 2:
                    sides.append((east - west, north - south))
                new = keep * here[f] + spread * (state[f, k] + state[f, k + 2])
                new = new + (to_west * west + to_east * east) + (to_south * south + to_north * north)
                if f == 0:
                    new = new + height * heat_in
                elif f == 1:
                    new = new + height * vapour_in
                else:
                    lift = sides[0][f - 2] + 0.6 * sides[1][f - 2]
                    new = new + (0.5 * lift_gain * air_delta) * lift
                result.append(new)
            return result

        if c < STEPS - 1:

            def layer(k, carry, other=other, air_step=air_step):
                result = [jnp.where(inside, new, 0.0) for new in air_step(k)]
                for f in range(4):
                    other[f, k + 1] = result[f]
                weight = weights_ref[1, k]
                return (carry[0] + weight * result[2], carry[1] + weight * result[3])

            wind = lax.fori_loop(0, LEVELS, layer, (nothing, nothing))
            state, other = other, state
        else:
            for k in range(bands):
                first = lax.rem(band + k, bands) * depth

                def final(l, carry, out=outs[k], first=first, air_step=air_step):
                    result = [new[:8] for new in air_step(first + l)]
                    for p in range(2):
                        out[2 * l + p] = jnp.where(lane < 64, result[2 * p], roll(result[2 * p + 1], 64, 1))
                    return carry

                lax.fori_loop(0, depth, final, 0)

    for j in range(tiles):
        level_out[:, j * LANES : (j + 1) * LANES] = lev_a[j, own : own + rows]
        fuel_out[:, j * LANES : (j + 1) * LANES] = fuel[j, own : own + rows]


def unpack_kernel(bands, at_ref, *refs):
    slots, out = refs[:bands], refs[bands]
    depth = out.shape[1]
    lane = iota((8, LANES), 1)
    for k in range(bands):
        source = lax.rem(at_ref[1] - k + bands, bands)
        odd = lax.rem(source, 2)
        cols = pl.ds(pl.multiple_of((source // 2) * LANES, LANES), LANES)
        mine = (lane >= 64 * odd) & (lane < 64 * odd + 64)

        def body(l, carry, slot=slots[k], odd=odd, cols=cols, mine=mine):
            for p in range(2):
                both = slot[2 * l + p]
                for f in range(2):
                    shift = 64 * odd if f == 0 else 64 - 64 * odd
                    old = out[2 * p + f, l, :, cols]
                    out[2 * p + f, l, :, cols] = jnp.where(mine, roll(both, shift, 1), old)
            return carry

        lax.fori_loop(0, depth, body, 0)


def shape(*dims):
    return jax.ShapeDtypeStruct(dims, jnp.float32)


def vmem():
    return pl.BlockSpec(memory_space=pltpu.VMEM)


def smem():
    return pl.BlockSpec(memory_space=pltpu.SMEM)


def local(
    air_state,
    fire_level,
    fuel_left,
    fuel_class,
    ignition,
    plan,
    spread_rate,
    burn_time,
    heat_content,
    moisture_content,
):
    tables = jnp.stack([spread_rate, burn_time, heat_content, moisture_content])
    weights = np.stack(level_weights(LEVELS))
    bands = lax.axis_size(BANDS)
    tile_count = lax.axis_size("tile")
    at = jnp.stack([lax.axis_index("tile"), lax.axis_index(BANDS), tile_count]).astype(jnp.int32)
    depth = air_state.shape[1]
    rows, width = fire_level.shape
    tiles = width // LANES
    count = air_tiles(depth)
    extra = 2 * (rows // 8)
    params = pltpu.CompilerParams(vmem_limit_bytes=VMEM_LIMIT)

    sizes = [count + (extra if k in (1, bands - 1) else 0) for k in range(bands)]
    packed = pl.pallas_call(
        functools.partial(pack_kernel, bands),
        out_shape=[shape(size, 8, LANES) for size in sizes] + [shape(4, tiles, EDGE, LANES)] * 2,
        in_specs=[smem()] + [vmem()] * 5,
        out_specs=[vmem()] * (bands + 2),
        compiler_params=params,
        name="pack",
    )(at, air_state, fire_level, fuel_left, fuel_class, ignition)
    slots, up, down = packed[:bands], packed[bands], packed[bands + 1]

    rise = [(i, i + 1) for i in range(tile_count - 1)]
    sink = [(j, i) for i, j in rise]

    def turn(values):
        moved = [values[0]]
        for k in range(1, bands):
            moved.append(lax.ppermute(values[k], BANDS, [(i, (i + k) % bands) for i in range(bands)]))
        return moved

    fire_up = lax.ppermute(down, "tile", rise)
    fire_down = lax.ppermute(up, "tile", sink)
    slots = turn(slots)
    edges = (bands // 2) * count + 4 * (EDGE // 8)
    up, down = pl.pallas_call(
        functools.partial(relay_kernel, bands, rows),
        out_shape=[shape(edges, 8, LANES)] * 2,
        in_specs=[vmem()] * bands,
        out_specs=[vmem()] * 2,
        compiler_params=params,
        name="relay",
    )(*slots)
    edge_up = lax.ppermute(down, "tile", rise)
    edge_down = lax.ppermute(up, "tile", sink)

    span = rows + 2 * EDGE
    fire = pltpu.VMEM((tiles + 1, span + 2 * PAD, LANES), jnp.float32)
    flat = pltpu.VMEM((tiles + 1, span, LANES), jnp.float32)
    atmosphere = pltpu.VMEM((4, LEVELS + 2, 16, LANES), jnp.float32)
    results = pl.pallas_call(
        functools.partial(main_kernel, bands),
        out_shape=[shape(rows, width)] * 2 + [shape(2 * depth, 8, LANES)] * bands,
        in_specs=[smem()] * 4 + [vmem()] * (4 + bands + 4),
        out_specs=[vmem()] * (2 + bands),
        scratch_shapes=[fire] * 9 + [flat] * 4 + [atmosphere] * 2,
        compiler_params=params,
        name="window",
    )(
        at,
        plan,
        tables,
        weights,
        fire_level,
        fuel_left,
        fuel_class,
        ignition,
        *slots,
        fire_up,
        fire_down,
        edge_up,
        edge_down,
    )
    level_out, fuel_out = results[:2]
    slabs = turn(results[2:])
    air_out = pl.pallas_call(
        functools.partial(unpack_kernel, bands),
        out_shape=shape(*air_state.shape),
        in_specs=[smem()] + [vmem()] * bands,
        out_specs=vmem(),
        compiler_params=params,
        name="unpack",
    )(at, *slabs)
    return (air_out, level_out, fuel_out)


def solution(mesh):
    placed = (
        P(None, ("sect", "sub"), ("group", "tile"), None),
        P(("group", "tile"), ("sect", "sub")),
        P(("group", "tile"), ("sect", "sub")),
        P(("group", "tile"), ("sect", "sub")),
        P(("group", "tile"), ("sect", "sub")),
        P(),
        P(),
        P(),
        P(),
        P(),
    )
    return jax.shard_map(
        local,
        mesh=mesh,
        in_specs=placed,
        out_specs=(
            P(None, ("sect", "sub"), ("group", "tile"), None),
            P(("group", "tile"), ("sect", "sub")),
            P(("group", "tile"), ("sect", "sub")),
        ),
        check_vma=False,
    )
```

```python
import functools
import math

import jax
import jax.numpy as jnp
from jax import lax
from jax.experimental import pallas as pl
from jax.experimental.pallas import tpu as pltpu
from jax.sharding import PartitionSpec as P

LEVELS = 80
REFINE = 10
STEPS = 4
SUBSTEPS = 4
NFUEL = 13

LANES = 128
HALO = STEPS
EDGE = HALO * REFINE
PAD = 8

air_delta = 0.1
diffusion = 0.2
heat_gain = 20.0
vapour_gain = 20.0
lift_gain = 0.3
wind_gain = 0.5
fire_delta = 0.15

BANDS = ("sect", "sub")
UNROLL_LOOKUP = 4
UNROLL_FIRE = 8
UNROLL_AIR = 8
UNROLL_FINAL = 10
RELAY_FLOPS = 5 * 10**9
SURVEY_FLOPS = 10**10
PACK_LIMIT = 62 * 1024 * 1024
VMEM_LIMIT = 40 * 1024 * 1024


def iota(shape, dim):
    return lax.broadcasted_iota(jnp.int32, shape, dim)


def roll(value, shift, axis):
    return pltpu.roll(value, shift, axis)


def unrolled(low, high, step, body, carry):
    def group(i, carry):
        for n in range(step):
            carry = body(low + i * step + n, carry)
        return carry

    whole = (high - low) // step
    carry = lax.fori_loop(0, whole, group, carry)
    for i in range(low + whole * step, high):
        carry = body(i, carry)
    return carry


def level_weight(k, rate, total):
    scale = total / sum(math.exp(-rate * j / LEVELS) for j in range(LEVELS))
    height = jnp.full((8, LANES), k, jnp.int32).astype(jnp.float32)
    return jnp.exp(height * (-rate / LEVELS)) * scale


def band_index():
    return lax.axis_index("sect") * lax.axis_size("sub") + lax.axis_index("sub")


def air_tiles(depth):
    return 2 * depth + -(-depth // 3)


def pack_kernel(bands, *refs):
    sources, outs, scratch, sems = refs[:5], refs[5 : bands + 7], refs[bands + 7 : bands + 12], refs[bands + 12]
    slots, up_ref, down_ref = outs[:bands], outs[bands], outs[bands + 1]
    copies = [pltpu.make_async_copy(a, b, sems.at[n]) for n, (a, b) in enumerate(zip(sources, scratch))]
    for copy in copies:
        copy.start()
    for copy in copies:
        copy.wait()
    air_ref, level_ref, fuel_ref, class_ref, ignite_ref = scratch
    depth = air_ref.shape[1]
    lane_tiles = air_ref.shape[3] // LANES
    rows, width = level_ref.shape
    lane = iota((8, LANES), 1)
    fields = [ref[...] for ref in (level_ref, fuel_ref)]
    fields += [ref[...].astype(jnp.float32) for ref in (class_ref, ignite_ref)]
    for a, field in enumerate(fields):
        for j in range(width // LANES):
            cols = field[:, j * LANES : (j + 1) * LANES]
            up_ref[a, j] = cols[:EDGE]
            down_ref[a, j] = cols[rows - EDGE :]
    base = air_tiles(depth)
    wide = iota((rows, LANES), 1)
    for pair in range(2):
        first, second = fields[2 * pair], fields[2 * pair + 1]
        at = pl.ds(base + pair * (rows // 8), rows // 8)
        to_next = jnp.where(wide < 64, roll(second[:, width - LANES :], 64, 1), first[:, width - LANES :])
        slots[1][at] = to_next.reshape(rows // 8, 8, LANES)
        to_prev = jnp.where(wide < 64, first[:, :LANES], roll(second[:, :LANES], 64, 1))
        slots[bands - 1][at] = to_prev.reshape(rows // 8, 8, LANES)
    band = band_index()
    for k in range(bands):
        dest = lax.rem(band + k, bands)
        odd = lax.rem(dest, 2)
        own = pl.multiple_of((dest // 2) * LANES, LANES)
        high = (dest + 1) // 2
        right = pl.multiple_of(jnp.minimum(high, lane_tiles - 1) * LANES, LANES)
        left = pl.multiple_of(jnp.maximum(high - 1, 0) * LANES, LANES)
        turn = 64 * odd
        back = 64 - turn
        from_right = lane < 96 - turn
        for l in range(depth):
            for p in range(2):
                first = air_ref[2 * p, l, :, pl.ds(own, LANES)]
                second = air_ref[2 * p + 1, l, :, pl.ds(own, LANES)]
                slots[k][2 * l + p] = jnp.where(lane < 64, roll(first, turn, 1), roll(second, back, 1))
        for g in range(-(-depth // 3)):
            packed = jnp.zeros((8, LANES), jnp.float32)
            for l in range(3 * g, min(3 * g + 3, depth)):
                for f in range(4):
                    j = (l - 3 * g) * 4 + f
                    edge = jnp.where(
                        from_right, air_ref[f, l, :, pl.ds(right, LANES)], air_ref[f, l, :, pl.ds(left, LANES)]
                    )
                    edge = roll(edge, 4 * j + back, 1)
                    here = ((lane >= 4 * j) & (lane < 4 * j + 4)) | ((lane >= 60 + 4 * j) & (lane < 64 + 4 * j))
                    packed = jnp.where(here, edge, packed)
            slots[k][2 * depth + g] = packed


def corner_tiles(next_ref, prev_ref, base, rows):
    lane = iota((rows, LANES), 1)
    result = []
    for pair in range(2):
        at = pl.ds(base + pair * (rows // 8), rows // 8)
        left = prev_ref[at].reshape(rows, LANES)
        right = next_ref[at].reshape(rows, LANES)
        result.append(jnp.where(lane < 64, right, left))
        result.append(roll(jnp.where(lane < 64, left, right), 64, 1))
    return result


def relay_kernel(bands, rows, *refs):
    slots, up_ref, down_ref = refs[:bands], refs[bands], refs[bands + 1]
    tiles = slots[0].shape[0]
    sub = iota((8, LANES), 0)
    for half in range(bands // 2):
        one, two = slots[2 * half], slots[2 * half + 1]

        def body(i, carry, one=one, two=two, half=half):
            first, second = one[i], two[i]
            up_ref[half * tiles + i] = jnp.where(sub < 4, first, roll(second, 4, 0))
            down_ref[half * tiles + i] = jnp.where(sub < 4, roll(first, 4, 0), second)
            return carry

        unrolled(0, tiles, 8, body, 0)
    corners = corner_tiles(slots[bands - 1], slots[1], tiles, rows)
    base = (bands // 2) * tiles
    count = EDGE // 8
    for a, corner in enumerate(corners):
        at = pl.ds(base + a * count, count)
        up_ref[at] = corner[:EDGE].reshape(count, 8, LANES)
        down_ref[at] = corner[rows - EDGE :].reshape(count, 8, LANES)


def table_vectors(tables_ref):
    lane = iota((8, LANES), 1)
    vectors = []
    for n in range(4):
        vector = jnp.zeros((8, LANES), jnp.float32)
        for category in range(NFUEL):
            vector = jnp.where(lane == category, tables_ref[n, category], vector)
        vectors.append(vector)
    vectors[1] = -1.0 / jnp.where(lane < NFUEL, vectors[1], 1.0)
    return vectors


def pick(vector, index):
    return jnp.take_along_axis(vector, index, axis=1, mode="promise_in_bounds")


def survey_kernel(tables_ref, class_ref, up_ref, down_ref, *outs):
    vectors = table_vectors(tables_ref)
    rows, width = class_ref.shape
    tiles = width // LANES

    def fill(first, count, read):
        def body(t, carry):
            for j in range(tiles):
                index = read(j, pl.ds(pl.multiple_of(8 * t, 8), 8)).astype(jnp.int32)
                for vector, out in zip(vectors, outs):
                    out[j, pl.ds(pl.multiple_of(first + 8 * t, 8), 8)] = pick(vector, index)
            return carry

        unrolled(0, count // 8, 5, body, 0)

    fill(0, EDGE, lambda j, at: up_ref[2, j, at])
    fill(EDGE, rows, lambda j, at: class_ref[at, j * LANES : (j + 1) * LANES])
    fill(EDGE + rows, EDGE, lambda j, at: down_ref[2, j, at])


def main_kernel(bands, plan_ref, tables_ref, level_in, fuel_in, ignite_in, *refs):
    slots = refs[:bands]
    fire_up, fire_down, edge_up, edge_down = refs[bands : bands + 4]
    values_in = refs[bands + 4 : bands + 8]
    level_out, fuel_out = refs[bands + 8 : bands + 10]
    outs = refs[bands + 10 : 2 * bands + 10]
    scratch = list(refs[2 * bands + 10 :])
    lev_a, lev_b, fuel, ignite = scratch[:4]
    pace, burnt, wind_u, wind_v, energy, vapour, air_a, air_b = scratch[4:12]
    values_side = scratch[12:]
    tile, band, tile_count = lax.axis_index("tile"), band_index(), lax.axis_size("tile")
    rows, width = level_in.shape
    tiles = width // LANES
    depth = LEVELS // bands
    count = air_tiles(depth)
    own = PAD + EDGE
    span = rows + 2 * EDGE
    lane = iota((8, LANES), 1)
    first_tile, final_tile = tile == 0, tile == tile_count - 1
    first_band, final_band = band == 0, band == bands - 1

    def strip(t, base=PAD):
        return pl.ds(pl.multiple_of(base + 8 * t, 8), 8)

    corners = corner_tiles(slots[bands - 1], slots[1], count, rows)
    base = (bands // 2) * count
    sides = []
    for a, (source, held) in enumerate(((level_in, lev_a), (fuel_in, fuel), (None, None), (ignite_in, ignite))):
        at = pl.ds(base + a * (EDGE // 8), EDGE // 8)
        upper, lower = edge_up[at].reshape(EDGE, LANES), edge_down[at].reshape(EDGE, LANES)
        if held is None:
            side = jnp.concatenate([upper, corners[a], lower], axis=0).astype(jnp.int32)
            vectors = table_vectors(tables_ref)
            for n in range(span // 8):
                for vector, out in zip(vectors, values_side):
                    out[8 * n : 8 * n + 8] = pick(vector, side[8 * n : 8 * n + 8])
            continue
        for j in range(tiles):
            held[j, PAD:own] = fire_up[a, j]
            held[j, own : own + rows] = source[:, j * LANES : (j + 1) * LANES].astype(jnp.float32)
            held[j, own + rows : own + rows + EDGE] = fire_down[a, j]
        held[tiles, PAD:own] = upper
        held[tiles, own : own + rows] = corners[a]
        held[tiles, own + rows : own + rows + EDGE] = lower

    def value_at(n, j, t):
        return values_in[n][j, strip(t, 0)] if j < tiles else values_side[n][strip(t, 0)]

    spare = jnp.zeros((tiles + 1, PAD, LANES), jnp.float32)
    for held in (lev_a, lev_b):
        held[:, :PAD] = spare
        held[:, PAD + span :] = spare

    def kindled(values, t, c):
        return [
            jnp.where(ignite[j, strip(t)] <= c, jnp.minimum(value, -1.0), value) for j, value in enumerate(values)
        ]

    mend_low = first_band & (lane == LANES - 1)
    mend_high = final_band & (lane == 0)

    def mend_lanes(values):
        halo = jnp.where(mend_low, roll(values[0], LANES - 1, 1), values[tiles])
        halo = jnp.where(mend_high, roll(values[tiles - 1], 1, 1), halo)
        return values[:tiles] + [halo]

    def mend_rows(held):
        @pl.when(first_tile)
        def _():
            for j in range(tiles + 1):
                held[j, own - 1 : own] = held[j, own : own + 1]

        @pl.when(final_tile)
        def _():
            for j in range(tiles + 1):
                held[j, own + rows : own + rows + 1] = held[j, own + rows - 1 : own + rows]

    def kindle(t, carry):
        values = mend_lanes(kindled([lev_a[j, strip(t)] for j in range(tiles + 1)], t, 0))
        for j, value in enumerate(values):
            lev_a[j, strip(t)] = value
        return carry

    unrolled(0, span // 8, UNROLL_LOOKUP, kindle, 0)
    mend_rows(lev_a)

    sub = iota((8, LANES), 0)
    low_row = jnp.where(final_tile, 0, 4)
    high_row = jnp.where(first_tile, 8, 4)
    low_lane = jnp.where(final_band, 64, 68)
    high_lane = jnp.where(first_band, 128, 124)
    inside_own = (lane < low_lane) | (lane >= high_lane)
    inside = (inside_own, inside_own & ((sub < low_row) | (sub >= high_row)))

    def layer_at(k, part, shift=0):
        return pl.ds(pl.multiple_of((k + 1) * 24 + 8 * part, 8) + shift, 8)

    def put(held, f, k, part, value):
        held[f, layer_at(k, part)] = value
        if part == 2:
            held[f, layer_at(k, 0)] = value

    for k in range(bands):
        source = lax.rem(band - k + bands, bands)
        half = k // 2

        def whole(i, k=k, half=half):
            below, above = edge_down[half * count + i], edge_up[half * count + i]
            if k % 2 == 0:
                halo = jnp.where(sub < 4, below, roll(above, 4, 0))
            else:
                halo = jnp.where(sub < 4, roll(below, 4, 0), above)
            return slots[k][i], halo

        for g in range(-(-depth // 3)):
            edges = whole(2 * depth + g)
            for l in range(3 * g, min(3 * g + 3, depth)):
                for p in range(2):
                    both = whole(2 * l + p)
                    for f in range(2):
                        j = (l - 3 * g) * 4 + 2 * p + f
                        for part in range(2):
                            inner = both[part] if f == 0 else roll(both[part], 64, 1)
                            value = jnp.where(lane < 64, inner, roll(edges[part], 64 - 4 * j, 1))
                            value = jnp.where(inside[part], value, 0.0)
                            put(air_a, 2 * p + f, source * depth + l, part + 1, value)
    nothing = jnp.zeros((8, LANES), jnp.float32)
    for held in (air_a, air_b):
        for f in range(4):
            for part in range(3):
                held[f, layer_at(-1, part)] = nothing
                held[f, layer_at(LEVELS, part)] = nothing

    cell, column = iota((LANES, LANES), 0), iota((LANES, LANES), 1)
    start = jnp.where(
        column < 64 + HALO,
        REFINE * column,
        jnp.where(column >= LANES - HALO, REFINE * column + (tiles + 1) * LANES - REFINE * LANES, -LANES * 1000),
    )
    across = []
    for j in range(tiles + 1):
        place = cell + j * LANES
        across.append(jnp.where((place >= start) & (place < start + REFINE), 1.0, 0.0).astype(jnp.bfloat16))
    outward = [jnp.concatenate([matrix] * 2, axis=1) for matrix in across]
    across = [jnp.concatenate([matrix] * 2, axis=0) for matrix in across]
    cell, column = iota((span, 16), 0), iota((span, 16), 1)
    start = jnp.where(column < 8 + HALO, EDGE + REFINE * column, REFINE * (column - 12))
    along = jnp.where((cell >= start) & (cell < start + REFINE), 1.0, 0.0).astype(jnp.float32)

    def parts(value, axis):
        high = value.astype(jnp.bfloat16)
        low = (value - high.astype(jnp.float32)).astype(jnp.bfloat16)
        return jnp.concatenate([high, low], axis=axis)

    def dot(a, b, dims):
        return lax.dot_general(a, b, (dims, ((), ())), preferred_element_type=jnp.float32)

    def blow(total, k, result):
        weight = level_weight(k, 1.0, 1.0)
        return [a + weight * b for a, b in zip(total, result)]

    def first_wind(k, carry):
        return blow(carry, k, [air_a[f, layer_at(k, part)] for f in (2, 3) for part in (1, 2)])

    calm = [nothing] * 4
    wind = unrolled(0, LEVELS, UNROLL_AIR, first_wind, calm)

    spread = air_delta * diffusion
    mixing = [jnp.where(mask, spread, 0.0) for mask in inside]
    lifting = [jnp.where(mask, 0.5 * lift_gain * air_delta, 0.0) for mask in inside]
    lifting = [(value, 0.6 * value) for value in lifting]
    state, other = air_a, air_b
    for c in range(STEPS):
        reach = EDGE - REFINE * (c + 1)
        fire_step = plan_ref[c].astype(jnp.float32) * fire_delta

        def strips(margin):
            return (EDGE - margin) // 8, -(-(EDGE + rows + margin) // 8)

        low, high = (8 * t for t in strips(reach + SUBSTEPS - 1))
        spread_rows = jnp.concatenate([along[low:high].astype(jnp.bfloat16)] * 2, axis=1)
        coarse = parts(jnp.concatenate(wind, axis=0) * wind_gain, 1)
        for j in range(tiles + 1):
            wide = parts(dot(coarse, outward[j], ((1,), (1,))).reshape(2, 16, LANES), 1)
            wind_u[j, low:high] = dot(spread_rows, wide[0], ((1,), (0,)))
            wind_v[j, low:high] = dot(spread_rows, wide[1], ((1,), (0,)))

        before, after = lev_a, lev_b
        for s in range(SUBSTEPS):

            def advance(t, carry, c=c, s=s, fire_step=fire_step, before=before, after=after):
                row = pl.multiple_of(PAD + 8 * t, 8)
                at, flat = strip(t), strip(t, 0)
                centre = [before[j, at] for j in range(tiles + 1)]
                lower = [roll(value, 1, 1) for value in centre]
                upper = [roll(value, LANES - 1, 1) for value in centre]
                result = []
                for j in range(tiles + 1):
                    west = before[j, pl.ds(row - 1, 8)]
                    east = before[j, pl.ds(row + 1, 8)]
                    south = jnp.where(lane == 0, lower[j - 1], lower[j])
                    north = jnp.where(lane == LANES - 1, upper[(j + 1) % (tiles + 1)], upper[j])
                    here = centre[j]
                    back, ahead = here - west, east - here
                    below, above = here - south, north - here
                    a, b = jnp.maximum(back, 0.0), jnp.minimum(ahead, 0.0)
                    d, e = jnp.maximum(below, 0.0), jnp.minimum(above, 0.0)
                    square = (a * a + b * b) + (d * d + e * e)
                    steep = square * lax.rsqrt(jnp.maximum(square, 1.2e-38))
                    gx, gy = back + ahead, below + above
                    tail = (wind_u[j, flat] * gx + wind_v[j, flat] * gy) * lax.rsqrt((gx * gx + 4.0) + gy * gy)
                    if s == 0:
                        speed = fire_step * value_at(0, j, t)
                        pace[j, flat] = speed
                    else:
                        speed = pace[j, flat]
                    result.append(here - (speed * (1.0 + jnp.maximum(tail, 0.0))) * steep)
                for j in range(tiles + 1):
                    unburnt = jnp.clip(result[j], -0.5, 0.5)
                    if s > 0:
                        unburnt = unburnt + burnt[j, flat]
                    if s < SUBSTEPS - 1:
                        burnt[j, flat] = unburnt
                    else:
                        held = fuel[j, at]
                        remain = held * jnp.exp((0.5 * SUBSTEPS - unburnt) * (fire_step * value_at(1, j, t)))
                        spent = held - remain
                        fuel[j, at] = remain
                        energy[j, flat] = spent * value_at(2, j, t)
                        vapour[j, flat] = spent * value_at(3, j, t)
                if s == SUBSTEPS - 1 and c < STEPS - 1:
                    result = kindled(result, t, c + 1)
                for j, value in enumerate(mend_lanes(result)):
                    after[j, at] = value
                return carry

            unrolled(*strips(reach + SUBSTEPS - 1 - s), UNROLL_FIRE, advance, 0)
            mend_rows(after)
            before, after = after, before

        low, high = (8 * t for t in strips(reach))
        gather_rows = along[low:high].astype(jnp.bfloat16)
        forcing = []
        for held, gain in ((energy, heat_gain), (vapour, vapour_gain)):
            total = dot(parts(held[0, low:high], 1), across[0], ((1,), (0,)))
            for j in range(1, tiles + 1):
                total = total + dot(parts(held[j, low:high], 1), across[j], ((1,), (0,)))
            both = dot(gather_rows, parts(total, 1), ((0,), (0,)))
            flux = (both[:, :LANES] + both[:, LANES:]) * (air_delta * gain / (REFINE * REFINE))
            forcing.append([jnp.where(inside[part], flux[8 * part : 8 * part + 8], 0.0) for part in range(2)])

        def air_step(k, part, state=state, forcing=forcing):
            at = layer_at(k, part + 1)
            here = [state[f, at] for f in range(4)]
            west = [state[f, layer_at(k, part + 1, -1)] for f in range(4)]
            east = [state[f, layer_at(k, 1 if part == 0 else 0, 1)] for f in range(4)]
            south = [roll(value, 1, 1) for value in here]
            north = [roll(value, LANES - 1, 1) for value in here]
            u, v = air_delta * here[2], air_delta * here[3]
            mix = mixing[part]
            to_west, to_east = mix + jnp.maximum(u, 0.0), mix - jnp.minimum(u, 0.0)
            to_south, to_north = mix + jnp.maximum(v, 0.0), mix - jnp.minimum(v, 0.0)
            keep = (1.0 - 6.0 * spread) - (jnp.abs(u) + jnp.abs(v))
            height = level_weight(k, 2.0, float(LEVELS))
            result = []
            for f in range(4):
                new = keep * here[f] + mix * (state[f, layer_at(k - 1, part + 1)] + state[f, layer_at(k + 1, part + 1)])
                new = new + (to_west * west[f] + to_east * east[f]) + (to_south * south[f] + to_north * north[f])
                if f < 2:
                    new = new + height * forcing[f][part]
                else:
                    low, high = (west, east) if f == 2 else (south, north)
                    new = new + (lifting[part][0] * (high[0] - low[0]) + lifting[part][1] * (high[1] - low[1]))
                result.append(new)
            return result

        if c < STEPS - 1:

            def layer(k, carry, other=other, air_step=air_step):
                result = [air_step(k, part) for part in range(2)]
                for part in range(2):
                    for f in range(4):
                        put(other, f, k, part + 1, result[part][f])
                return blow(carry, k, [result[part][f] for f in (2, 3) for part in range(2)])

            wind = unrolled(0, LEVELS, UNROLL_AIR, layer, calm)
            state, other = other, state
        else:
            for k in range(bands):
                first = lax.rem(band + k, bands) * depth

                def final(l, carry, out=outs[k], first=first, air_step=air_step):
                    result = air_step(first + l, 0)
                    for p in range(2):
                        out[2 * l + p] = jnp.where(lane < 64, result[2 * p], roll(result[2 * p + 1], 64, 1))
                    return carry

                unrolled(0, depth, UNROLL_FINAL, final, 0)

    for j in range(tiles):
        level_out[:, j * LANES : (j + 1) * LANES] = lev_a[j, own : own + rows]
        fuel_out[:, j * LANES : (j + 1) * LANES] = fuel[j, own : own + rows]


def unpack_kernel(bands, *refs):
    slots, out = refs[:bands], refs[bands]
    depth = out.shape[1]
    lane = iota((8, LANES), 1)
    for k in range(bands):
        source = lax.rem(band_index() - k + bands, bands)
        odd = lax.rem(source, 2)
        cols = pl.ds(pl.multiple_of((source // 2) * LANES, LANES), LANES)
        mine = (lane >= 64 * odd) & (lane < 64 * odd + 64)

        def body(l, carry, slot=slots[k], odd=odd, cols=cols, mine=mine):
            for p in range(2):
                both = slot[2 * l + p]
                for f in range(2):
                    shift = 64 * odd if f == 0 else 64 - 64 * odd
                    old = out[2 * p + f, l, :, cols]
                    out[2 * p + f, l, :, cols] = jnp.where(mine, roll(both, shift, 1), old)
            return carry

        unrolled(0, depth, 10, body, 0)


def shape(*dims):
    return jax.ShapeDtypeStruct(dims, jnp.float32)


def vmem():
    return pl.BlockSpec(memory_space=pltpu.VMEM)


def smem():
    return pl.BlockSpec(memory_space=pltpu.SMEM)


def local(
    air_state,
    fire_level,
    fuel_left,
    fuel_class,
    ignition,
    plan,
    spread_rate,
    burn_time,
    heat_content,
    moisture_content,
):
    tables = jnp.stack([spread_rate, burn_time, heat_content, moisture_content])
    bands = lax.axis_size(BANDS)
    tile_count = lax.axis_size("tile")
    depth = air_state.shape[1]
    rows, width = fire_level.shape
    tiles = width // LANES
    count = air_tiles(depth)
    extra = 2 * (rows // 8)
    params = pltpu.CompilerParams(vmem_limit_bytes=VMEM_LIMIT)

    sizes = [count + (extra if k in (1, bands - 1) else 0) for k in range(bands)]
    packed = pl.pallas_call(
        functools.partial(pack_kernel, bands),
        out_shape=[shape(size, 8, LANES) for size in sizes] + [shape(4, tiles, EDGE, LANES)] * 2,
        in_specs=[pl.BlockSpec(memory_space=pltpu.HBM)] * 5,
        out_specs=[vmem()] * (bands + 2),
        scratch_shapes=[
            pltpu.VMEM(x.shape, x.dtype) for x in (air_state, fire_level, fuel_left, fuel_class, ignition)
        ]
        + [pltpu.SemaphoreType.DMA((5,))],
        compiler_params=pltpu.CompilerParams(vmem_limit_bytes=PACK_LIMIT),
        name="pack",
    )(air_state, fire_level, fuel_left, fuel_class, ignition)
    slots, up, down = packed[:bands], packed[bands], packed[bands + 1]

    rise = [(i, i + 1) for i in range(tile_count - 1)]
    sink = [(j, i) for i, j in rise]

    def turn(values):
        moved = [values[0]]
        for k in range(1, bands):
            moved.append(lax.ppermute(values[k], BANDS, [(i, (i + k) % bands) for i in range(bands)]))
        return moved

    fire_up = lax.ppermute(down, "tile", rise)
    fire_down = lax.ppermute(up, "tile", sink)
    slots = turn(slots)
    edges = (bands // 2) * count + 4 * (EDGE // 8)
    up, down = pl.pallas_call(
        functools.partial(relay_kernel, bands, rows),
        out_shape=[shape(edges, 8, LANES)] * 2,
        in_specs=[vmem()] * bands,
        out_specs=[vmem()] * 2,
        compiler_params=params,
        cost_estimate=pl.CostEstimate(flops=RELAY_FLOPS, bytes_accessed=0, transcendentals=0),
        name="relay",
    )(*slots)
    edge_up = lax.ppermute(down, "tile", rise)
    edge_down = lax.ppermute(up, "tile", sink)

    span = rows + 2 * EDGE
    values = pl.pallas_call(
        survey_kernel,
        out_shape=[shape(tiles, span, LANES)] * 4,
        in_specs=[smem()] + [vmem()] * 3,
        out_specs=[vmem()] * 4,
        compiler_params=params,
        cost_estimate=pl.CostEstimate(flops=SURVEY_FLOPS, bytes_accessed=0, transcendentals=0),
        name="survey",
    )(tables, fuel_class, fire_up, fire_down)
    fire = pltpu.VMEM((tiles + 1, span + 2 * PAD, LANES), jnp.float32)
    flat = pltpu.VMEM((tiles + 1, span, LANES), jnp.float32)
    side = pltpu.VMEM((span, LANES), jnp.float32)
    atmosphere = pltpu.VMEM((4, (LEVELS + 2) * 24, LANES), jnp.float32)
    results = pl.pallas_call(
        functools.partial(main_kernel, bands),
        out_shape=[shape(rows, width)] * 2 + [shape(2 * depth, 8, LANES)] * bands,
        in_specs=[smem()] * 2 + [vmem()] * (3 + bands + 8),
        out_specs=[vmem()] * (2 + bands),
        scratch_shapes=[fire] * 4 + [flat] * 6 + [atmosphere] * 2 + [side] * 4,
        compiler_params=params,
        name="window",
    )(
        plan,
        tables,
        fire_level,
        fuel_left,
        ignition,
        *slots,
        fire_up,
        fire_down,
        edge_up,
        edge_down,
        *values,
    )
    level_out, fuel_out = results[:2]
    slabs = turn(results[2:])
    air_out = pl.pallas_call(
        functools.partial(unpack_kernel, bands),
        out_shape=shape(*air_state.shape),
        in_specs=[vmem()] * bands,
        out_specs=vmem(),
        compiler_params=params,
        name="unpack",
    )(*slabs)
    return (air_out, level_out, fuel_out)


def solution(mesh):
    placed = (
        P(None, ("sect", "sub"), ("group", "tile"), None),
        P(("group", "tile"), ("sect", "sub")),
        P(("group", "tile"), ("sect", "sub")),
        P(("group", "tile"), ("sect", "sub")),
        P(("group", "tile"), ("sect", "sub")),
        P(),
        P(),
        P(),
        P(),
        P(),
    )
    return jax.shard_map(
        local,
        mesh=mesh,
        in_specs=placed,
        out_specs=(
            P(None, ("sect", "sub"), ("group", "tile"), None),
            P(("group", "tile"), ("sect", "sub")),
            P(("group", "tile"), ("sect", "sub")),
        ),
        check_vma=False,
    )
```

```python
import functools
import math

import jax
import jax.numpy as jnp
from jax import lax
from jax.experimental import pallas as pl
from jax.experimental.pallas import tpu as pltpu
from jax.sharding import PartitionSpec as P

LEVELS = 80
REFINE = 10
STEPS = 4
SUBSTEPS = 4
NFUEL = 13

LANES = 128
HALO = STEPS
EDGE = HALO * REFINE
PAD = 8

air_delta = 0.1
diffusion = 0.2
heat_gain = 20.0
vapour_gain = 20.0
lift_gain = 0.3
wind_gain = 0.5
fire_delta = 0.15

BANDS = ("sect", "sub")
UNROLL_LOOKUP = 4
UNROLL_FIRE = 10
UNROLL_AIR = 16
UNROLL_FINAL = 10
KEEP_FLOPS = 10**9
RELAY_FLOPS = 5 * 10**9
SURVEY_FLOPS = 10**10
PACK_LIMIT = 62 * 1024 * 1024
VMEM_LIMIT = 40 * 1024 * 1024


def iota(shape, dim):
    return lax.broadcasted_iota(jnp.int32, shape, dim)


def roll(value, shift, axis):
    return pltpu.roll(value, shift, axis)


def unrolled(low, high, step, body, carry):
    def group(i, carry):
        for n in range(step):
            carry = body(low + i * step + n, carry)
        return carry

    groups = -(-(high - low) // step)
    step = -(-(high - low) // groups)
    whole = (high - low) // step
    carry = lax.fori_loop(0, whole, group, carry)
    for i in range(low + whole * step, high):
        carry = body(i, carry)
    return carry


def level_weights(rate, total):
    scale = total / sum(math.exp(-rate * j / LEVELS) for j in range(LEVELS))
    return jnp.exp(iota((LEVELS, LANES), 0).astype(jnp.float32) * (-rate / LEVELS)) * scale


def band_index():
    return lax.axis_index("sect") * lax.axis_size("sub") + lax.axis_index("sub")


def air_tiles(depth):
    return 2 * depth + -(-depth // 3)


def pack_slot(bands, k, air_ref, slot):
    depth = air_ref.shape[1]
    lane_tiles = air_ref.shape[3] // LANES
    lane = iota((8, LANES), 1)
    dest = lax.rem(band_index() + k, bands)
    odd = lax.rem(dest, 2)
    own = pl.multiple_of((dest // 2) * LANES, LANES)
    high = (dest + 1) // 2
    right = pl.multiple_of(jnp.minimum(high, lane_tiles - 1) * LANES, LANES)
    left = pl.multiple_of(jnp.maximum(high - 1, 0) * LANES, LANES)
    turn = 64 * odd
    back = 64 - turn
    from_right = lane < 96 - turn
    for l in range(depth):
        for p in range(2):
            first = air_ref[2 * p, l, :, pl.ds(own, LANES)]
            second = air_ref[2 * p + 1, l, :, pl.ds(own, LANES)]
            slot[2 * l + p] = jnp.where(lane < 64, roll(first, turn, 1), roll(second, back, 1))
    for g in range(-(-depth // 3)):
        packed = jnp.zeros((8, LANES), jnp.float32)
        for l in range(3 * g, min(3 * g + 3, depth)):
            for f in range(4):
                j = (l - 3 * g) * 4 + f
                edge = jnp.where(
                    from_right, air_ref[f, l, :, pl.ds(right, LANES)], air_ref[f, l, :, pl.ds(left, LANES)]
                )
                edge = roll(edge, 4 * j + back, 1)
                here = ((lane >= 4 * j) & (lane < 4 * j + 4)) | ((lane >= 60 + 4 * j) & (lane < 64 + 4 * j))
                packed = jnp.where(here, edge, packed)
        slot[2 * depth + g] = packed


def pack_kernel(bands, *refs):
    sources, outs, scratch, sems = refs[:5], refs[5 : bands + 6], refs[bands + 6 : bands + 11], refs[bands + 11]
    slots, up_ref, down_ref = outs[: bands - 1], outs[bands - 1], outs[bands]
    copies = [pltpu.make_async_copy(a, b, sems.at[n]) for n, (a, b) in enumerate(zip(sources, scratch))]
    for copy in copies:
        copy.start()
    for copy in copies:
        copy.wait()
    air_ref, level_ref, fuel_ref, class_ref, ignite_ref = scratch
    depth = air_ref.shape[1]
    rows, width = level_ref.shape
    fields = [ref[...] for ref in (level_ref, fuel_ref)]
    fields += [ref[...].astype(jnp.float32) for ref in (class_ref, ignite_ref)]
    for a, field in enumerate(fields):
        for j in range(width // LANES):
            cols = field[:, j * LANES : (j + 1) * LANES]
            up_ref[a, j] = cols[:EDGE]
            down_ref[a, j] = cols[rows - EDGE :]
    base = air_tiles(depth)
    wide = iota((rows, LANES), 1)
    for pair in range(2):
        first, second = fields[2 * pair], fields[2 * pair + 1]
        at = pl.ds(base + pair * (rows // 8), rows // 8)
        to_next = jnp.where(wide < 64, roll(second[:, width - LANES :], 64, 1), first[:, width - LANES :])
        slots[0][at] = to_next.reshape(rows // 8, 8, LANES)
        to_prev = jnp.where(wide < 64, first[:, :LANES], roll(second[:, :LANES], 64, 1))
        slots[bands - 2][at] = to_prev.reshape(rows // 8, 8, LANES)
    for k in range(1, bands):
        pack_slot(bands, k, air_ref, slots[k - 1])


def keep_kernel(bands, air_ref, slot):
    pack_slot(bands, 0, air_ref, slot)


def corner_tiles(next_ref, prev_ref, base, rows):
    lane = iota((rows, LANES), 1)
    result = []
    for pair in range(2):
        at = pl.ds(base + pair * (rows // 8), rows // 8)
        left = prev_ref[at].reshape(rows, LANES)
        right = next_ref[at].reshape(rows, LANES)
        result.append(jnp.where(lane < 64, right, left))
        result.append(roll(jnp.where(lane < 64, left, right), 64, 1))
    return result


def relay_kernel(bands, rows, *refs):
    slots, up_ref, down_ref = refs[:bands], refs[bands], refs[bands + 1]
    tiles = slots[0].shape[0]
    sub = iota((8, LANES), 0)
    for half in range(bands // 2):
        one, two = slots[2 * half], slots[2 * half + 1]

        def body(i, carry, one=one, two=two, half=half):
            first, second = one[i], two[i]
            up_ref[half * tiles + i] = jnp.where(sub < 4, first, roll(second, 4, 0))
            down_ref[half * tiles + i] = jnp.where(sub < 4, roll(first, 4, 0), second)
            return carry

        unrolled(0, tiles, 8, body, 0)
    corners = corner_tiles(slots[bands - 1], slots[1], tiles, rows)
    base = (bands // 2) * tiles
    count = EDGE // 8
    for a, corner in enumerate(corners):
        at = pl.ds(base + a * count, count)
        up_ref[at] = corner[:EDGE].reshape(count, 8, LANES)
        down_ref[at] = corner[rows - EDGE :].reshape(count, 8, LANES)


def table_vectors(tables_ref):
    lane = iota((8, LANES), 1)
    vectors = []
    for n in range(4):
        vector = jnp.zeros((8, LANES), jnp.float32)
        for category in range(NFUEL):
            vector = jnp.where(lane == category, tables_ref[n, category], vector)
        vectors.append(vector)
    vectors[1] = -1.0 / jnp.where(lane < NFUEL, vectors[1], 1.0)
    return vectors


def pick(vector, index):
    return jnp.take_along_axis(vector, index, axis=1, mode="promise_in_bounds")


def survey_kernel(tables_ref, class_ref, up_ref, down_ref, *outs):
    vectors = table_vectors(tables_ref)
    rows, width = class_ref.shape
    tiles = width // LANES

    def fill(first, count, read):
        def body(t, carry):
            for j in range(tiles):
                index = read(j, pl.ds(pl.multiple_of(8 * t, 8), 8)).astype(jnp.int32)
                for vector, out in zip(vectors, outs):
                    out[j, pl.ds(pl.multiple_of(first + 8 * t, 8), 8)] = pick(vector, index)
            return carry

        unrolled(0, count // 8, 5, body, 0)

    fill(0, EDGE, lambda j, at: up_ref[2, j, at])
    fill(EDGE, rows, lambda j, at: class_ref[at, j * LANES : (j + 1) * LANES])
    fill(EDGE + rows, EDGE, lambda j, at: down_ref[2, j, at])


def main_kernel(bands, tables_ref, level_in, fuel_in, ignite_in, *refs):
    slots = refs[:bands]
    fire_up, fire_down, edge_up, edge_down = refs[bands : bands + 4]
    values_in = refs[bands + 4 : bands + 8]
    level_out, fuel_out = refs[bands + 8 : bands + 10]
    outs = refs[bands + 10 : 2 * bands + 10]
    scratch = list(refs[2 * bands + 10 :])
    lev_a, lev_b, fuel, ignite = scratch[:4]
    pace, burnt, wind_u, wind_v, energy, vapour, air_a, air_b = scratch[4:12]
    values_side = scratch[12:16]
    weights = scratch[16]
    tile, band, tile_count = lax.axis_index("tile"), band_index(), lax.axis_size("tile")
    rows, width = level_in.shape
    tiles = width // LANES
    depth = LEVELS // bands
    count = air_tiles(depth)
    own = PAD + EDGE
    span = rows + 2 * EDGE
    lane = iota((8, LANES), 1)
    first_tile, final_tile = tile == 0, tile == tile_count - 1
    first_band, final_band = band == 0, band == bands - 1

    def strip(t, base=PAD):
        return pl.ds(pl.multiple_of(base + 8 * t, 8), 8)

    corners = corner_tiles(slots[bands - 1], slots[1], count, rows)
    base = (bands // 2) * count
    sides = []
    for a, (source, held) in enumerate(((level_in, lev_a), (fuel_in, fuel), (None, None), (ignite_in, ignite))):
        at = pl.ds(base + a * (EDGE // 8), EDGE // 8)
        upper, lower = edge_up[at].reshape(EDGE, LANES), edge_down[at].reshape(EDGE, LANES)
        if held is None:
            side = jnp.concatenate([upper, corners[a], lower], axis=0).astype(jnp.int32)
            vectors = table_vectors(tables_ref)
            for n in range(span // 8):
                for vector, out in zip(vectors, values_side):
                    out[8 * n : 8 * n + 8] = pick(vector, side[8 * n : 8 * n + 8])
            continue
        for j in range(tiles):
            held[j, PAD:own] = fire_up[a, j]
            held[j, own : own + rows] = source[:, j * LANES : (j + 1) * LANES].astype(jnp.float32)
            held[j, own + rows : own + rows + EDGE] = fire_down[a, j]
        held[tiles, PAD:own] = upper
        held[tiles, own : own + rows] = corners[a]
        held[tiles, own + rows : own + rows + EDGE] = lower

    def value_at(n, j, t):
        return values_in[n][j, strip(t, 0)] if j < tiles else values_side[n][strip(t, 0)]

    spare = jnp.zeros((tiles + 1, PAD, LANES), jnp.float32)
    for held in (lev_a, lev_b):
        held[:, :PAD] = spare
        held[:, PAD + span :] = spare

    def kindled(values, t, c):
        return [
            jnp.where(ignite[j, strip(t)] <= c, jnp.minimum(value, -1.0), value) for j, value in enumerate(values)
        ]

    mend_low = first_band & (lane == LANES - 1)
    mend_high = final_band & (lane == 0)

    def mend_lanes(values):
        halo = jnp.where(mend_low, roll(values[0], LANES - 1, 1), values[tiles])
        halo = jnp.where(mend_high, roll(values[tiles - 1], 1, 1), halo)
        return values[:tiles] + [halo]

    def mend_rows(held):
        @pl.when(first_tile)
        def _():
            for j in range(tiles + 1):
                held[j, own - 1 : own] = held[j, own : own + 1]

        @pl.when(final_tile)
        def _():
            for j in range(tiles + 1):
                held[j, own + rows : own + rows + 1] = held[j, own + rows - 1 : own + rows]

    def kindle(t, carry):
        values = mend_lanes(kindled([lev_a[j, strip(t)] for j in range(tiles + 1)], t, 0))
        for j, value in enumerate(values):
            lev_a[j, strip(t)] = value
        return carry

    unrolled(0, span // 8, UNROLL_LOOKUP, kindle, 0)
    mend_rows(lev_a)

    sub = iota((8, LANES), 0)
    low_row = jnp.where(final_tile, 0, 4)
    high_row = jnp.where(first_tile, 8, 4)
    low_lane = jnp.where(final_band, 64, 68)
    high_lane = jnp.where(first_band, 128, 124)
    inside_own = (lane < low_lane) | (lane >= high_lane)
    inside = (inside_own, inside_own & ((sub < low_row) | (sub >= high_row)))

    def layer_at(k, part, shift=0):
        return pl.ds(pl.multiple_of((k + 1) * 24 + 8 * part, 8) + shift, 8)

    def put(held, f, k, part, value):
        held[f, layer_at(k, part)] = value
        if part == 2:
            held[f, layer_at(k, 0)] = value

    for k in range(bands):
        source = lax.rem(band - k + bands, bands)
        half = k // 2

        def whole(i, k=k, half=half):
            below, above = edge_down[half * count + i], edge_up[half * count + i]
            if k % 2 == 0:
                halo = jnp.where(sub < 4, below, roll(above, 4, 0))
            else:
                halo = jnp.where(sub < 4, roll(below, 4, 0), above)
            return slots[k][i], halo

        for g in range(-(-depth // 3)):
            edges = whole(2 * depth + g)
            for l in range(3 * g, min(3 * g + 3, depth)):
                for p in range(2):
                    both = whole(2 * l + p)
                    for f in range(2):
                        j = (l - 3 * g) * 4 + 2 * p + f
                        for part in range(2):
                            inner = both[part] if f == 0 else roll(both[part], 64, 1)
                            value = jnp.where(lane < 64, inner, roll(edges[part], 64 - 4 * j, 1))
                            value = jnp.where(inside[part], value, 0.0)
                            put(air_a, 2 * p + f, source * depth + l, part + 1, value)
    nothing = jnp.zeros((8, LANES), jnp.float32)
    for held in (air_a, air_b):
        for f in range(4):
            for part in range(3):
                held[f, layer_at(-1, part)] = nothing
                held[f, layer_at(LEVELS, part)] = nothing

    weights[0] = level_weights(2.0, float(LEVELS))
    weights[1] = level_weights(1.0, 1.0)
    for held in (energy, vapour):
        for j in range(tiles + 1):
            held[j, :8] = nothing
            held[j, span - 8 :] = nothing

    def covers(shape, cell_dim):
        cell, column = iota(shape, cell_dim), iota(shape, 1 - cell_dim)
        start = jnp.where(
            column < 64 + HALO,
            REFINE * column,
            jnp.where(column >= LANES - HALO, REFINE * column + (tiles + 1 - REFINE) * LANES, -LANES * 1000),
        )
        return jnp.where((cell >= start) & (cell < start + REFINE), 1.0, 0.0).astype(jnp.bfloat16)

    cells = (tiles + 1) * LANES
    to_cells = jnp.concatenate([covers((LANES, cells), 1)] * 2, axis=0)
    to_columns = jnp.concatenate([covers((cells, LANES), 0)] * 2, axis=0)

    def parts(value, axis):
        high = value.astype(jnp.bfloat16)
        low = (value - high.astype(jnp.float32)).astype(jnp.bfloat16)
        return jnp.concatenate([high, low], axis=axis)

    def dot(a, b):
        return jnp.dot(a, b, preferred_element_type=jnp.float32)

    def swap(a, b):
        a, b = roll(a, 4, 0), roll(b, 4, 0)
        return jnp.where(sub < 4, a, b), jnp.where(sub < 4, b, a)

    def blow(total, k, result):
        weight = weights[1, pl.ds(k, 1)]
        return [a + weight * b for a, b in zip(total, result)]

    def first_wind(k, carry):
        return blow(carry, k, [air_a[f, layer_at(k, part)] for f in (2, 3) for part in (1, 2)])

    calm = [nothing] * 4
    wind = unrolled(0, LEVELS, UNROLL_AIR, first_wind, calm)

    spread = air_delta * diffusion
    mixing = [jnp.where(mask, spread, 0.0) for mask in inside]
    lifting = [jnp.where(mask, 0.5 * lift_gain * air_delta, 0.0) for mask in inside]
    lifting = [(value, 0.6 * value) for value in lifting]
    state, other = air_a, air_b
    for c in range(STEPS):
        reach = EDGE - REFINE * (c + 1)
        fire_step = tables_ref[4, c]

        def strips(margin):
            return (EDGE - margin) // 8, -(-(EDGE + rows + margin) // 8)

        coarse = [half for n in range(2) for half in swap(wind[2 * n + 1], wind[2 * n])]
        wide = dot(parts(jnp.concatenate(coarse, axis=0) * wind_gain, 1), to_cells)
        for n, held in enumerate((wind_u, wind_v)):
            for j in range(tiles + 1):
                for half in range(2):
                    value = wide[16 * n + 8 * half : 16 * n + 8 * half + 8, j * LANES : (j + 1) * LANES]
                    for row in range(REFINE):
                        held[j, pl.ds(half * (span // 2) + row, 8, stride=REFINE)] = value

        before, after = lev_a, lev_b
        for s in range(SUBSTEPS):

            def advance(t, carry, c=c, s=s, fire_step=fire_step, before=before, after=after):
                row = pl.multiple_of(PAD + 8 * t, 8)
                at, flat = strip(t), strip(t, 0)
                centre = [before[j, at] for j in range(tiles + 1)]
                lower = [roll(value, 1, 1) for value in centre]
                upper = [roll(value, LANES - 1, 1) for value in centre]
                result = []
                for j in range(tiles + 1):
                    west = before[j, pl.ds(row - 1, 8)]
                    east = before[j, pl.ds(row + 1, 8)]
                    south = jnp.where(lane == 0, lower[j - 1], lower[j])
                    north = jnp.where(lane == LANES - 1, upper[(j + 1) % (tiles + 1)], upper[j])
                    here = centre[j]
                    back, ahead = here - west, east - here
                    below, above = here - south, north - here
                    a, b = jnp.maximum(back, 0.0), jnp.minimum(ahead, 0.0)
                    d, e = jnp.maximum(below, 0.0), jnp.minimum(above, 0.0)
                    square = (a * a + b * b) + (d * d + e * e)
                    steep = square * lax.rsqrt(jnp.maximum(square, 1.2e-38))
                    gx, gy = back + ahead, below + above
                    tail = (wind_u[j, flat] * gx + wind_v[j, flat] * gy) * lax.rsqrt((gx * gx + 4.0) + gy * gy)
                    if s == 0:
                        speed = fire_step * value_at(0, j, t)
                        pace[j, flat] = speed
                    else:
                        speed = pace[j, flat]
                    result.append(here - (speed * (1.0 + jnp.maximum(tail, 0.0))) * steep)
                for j in range(tiles + 1):
                    unburnt = jnp.clip(result[j], -0.5, 0.5)
                    if s > 0:
                        unburnt = unburnt + burnt[j, flat]
                    if s < SUBSTEPS - 1:
                        burnt[j, flat] = unburnt
                    else:
                        held = fuel[j, at]
                        remain = held * jnp.exp((0.5 * SUBSTEPS - unburnt) * (fire_step * value_at(1, j, t)))
                        spent = held - remain
                        fuel[j, at] = remain
                        energy[j, flat] = spent * value_at(2, j, t)
                        vapour[j, flat] = spent * value_at(3, j, t)
                if s == SUBSTEPS - 1 and c < STEPS - 1:
                    result = kindled(result, t, c + 1)
                for j, value in enumerate(mend_lanes(result)):
                    after[j, at] = value
                return carry

            unrolled(*strips(reach + SUBSTEPS - 1 - s), UNROLL_FIRE, advance, 0)
            mend_rows(after)
            before, after = after, before

        totals = []
        for held in (energy, vapour):
            for half in range(2):
                total = []
                for j in range(tiles + 1):
                    value = [held[j, pl.ds(half * (span // 2) + row, 8, stride=REFINE)] for row in range(REFINE)]
                    while len(value) > 1:
                        value = [sum(value[n : n + 2]) for n in range(0, len(value), 2)]
                    total.append(value[0])
                totals.append(jnp.concatenate(total, axis=1))
        flux = dot(parts(jnp.concatenate(totals, axis=0), 1), to_columns)
        forcing = []
        for n, gain in enumerate((heat_gain, vapour_gain)):
            first, second = (flux[16 * n + 8 * half : 16 * n + 8 * half + 8] for half in range(2))
            halo, inner = swap(second, first)
            scale = air_delta * gain / (REFINE * REFINE)
            forcing.append([jnp.where(mask, value * scale, 0.0) for mask, value in zip(inside, (inner, halo))])

        def air_step(k, part, height, state=state, forcing=forcing):
            at = layer_at(k, part + 1)
            here = [state[f, at] for f in range(4)]
            west = [state[f, layer_at(k, part + 1, -1)] for f in range(4)]
            east = [state[f, layer_at(k, 1 if part == 0 else 0, 1)] for f in range(4)]
            south = [roll(value, 1, 1) for value in here]
            north = [roll(value, LANES - 1, 1) for value in here]
            u, v = air_delta * here[2], air_delta * here[3]
            mix = mixing[part]
            to_west, to_east = mix + jnp.maximum(u, 0.0), mix - jnp.minimum(u, 0.0)
            to_south, to_north = mix + jnp.maximum(v, 0.0), mix - jnp.minimum(v, 0.0)
            keep = (1.0 - 6.0 * spread) - (jnp.abs(u) + jnp.abs(v))
            result = []
            for f in range(4):
                new = keep * here[f] + mix * (state[f, layer_at(k - 1, part + 1)] + state[f, layer_at(k + 1, part + 1)])
                new = new + (to_west * west[f] + to_east * east[f]) + (to_south * south[f] + to_north * north[f])
                if f < 2:
                    new = new + height * forcing[f][part]
                else:
                    low, high = (west, east) if f == 2 else (south, north)
                    new = new + (lifting[part][0] * (high[0] - low[0]) + lifting[part][1] * (high[1] - low[1]))
                result.append(new)
            return result

        if c < STEPS - 1:

            def layer(k, carry, other=other, air_step=air_step):
                height = weights[0, pl.ds(k, 1)]
                result = [air_step(k, part, height) for part in range(2)]
                for part in range(2):
                    for f in range(4):
                        put(other, f, k, part + 1, result[part][f])
                return blow(carry, k, [result[part][f] for f in (2, 3) for part in range(2)])

            wind = unrolled(0, LEVELS, UNROLL_AIR, layer, calm)
            state, other = other, state
        else:
            for k in range(bands):
                first = lax.rem(band + k, bands) * depth

                def final(l, carry, out=outs[k], first=first, air_step=air_step):
                    result = air_step(first + l, 0, weights[0, pl.ds(first + l, 1)])
                    for p in range(2):
                        out[2 * l + p] = jnp.where(lane < 64, result[2 * p], roll(result[2 * p + 1], 64, 1))
                    return carry

                unrolled(0, depth, UNROLL_FINAL, final, 0)

    for j in range(tiles):
        level_out[:, j * LANES : (j + 1) * LANES] = lev_a[j, own : own + rows]
        fuel_out[:, j * LANES : (j + 1) * LANES] = fuel[j, own : own + rows]


def unpack_kernel(bands, *refs):
    slots, out = refs[:bands], refs[bands]
    depth = out.shape[1]
    lane = iota((8, LANES), 1)
    for k in range(bands):
        source = lax.rem(band_index() - k + bands, bands)
        odd = lax.rem(source, 2)
        cols = pl.ds(pl.multiple_of((source // 2) * LANES, LANES), LANES)
        mine = (lane >= 64 * odd) & (lane < 64 * odd + 64)

        def body(l, carry, slot=slots[k], odd=odd, cols=cols, mine=mine):
            for p in range(2):
                both = slot[2 * l + p]
                for f in range(2):
                    shift = 64 * odd if f == 0 else 64 - 64 * odd
                    old = out[2 * p + f, l, :, cols]
                    out[2 * p + f, l, :, cols] = jnp.where(mine, roll(both, shift, 1), old)
            return carry

        unrolled(0, depth, 10, body, 0)


def shape(*dims):
    return jax.ShapeDtypeStruct(dims, jnp.float32)


def vmem():
    return pl.BlockSpec(memory_space=pltpu.VMEM)


def smem():
    return pl.BlockSpec(memory_space=pltpu.SMEM)


def local(
    air_state,
    fire_level,
    fuel_left,
    fuel_class,
    ignition,
    plan,
    spread_rate,
    burn_time,
    heat_content,
    moisture_content,
):
    steps = jnp.pad(plan.astype(jnp.float32) * fire_delta, (0, NFUEL - STEPS))
    tables = jnp.stack([spread_rate, burn_time, heat_content, moisture_content, steps])
    bands = lax.axis_size(BANDS)
    tile_count = lax.axis_size("tile")
    depth = air_state.shape[1]
    rows, width = fire_level.shape
    tiles = width // LANES
    count = air_tiles(depth)
    extra = 2 * (rows // 8)
    params = pltpu.CompilerParams(vmem_limit_bytes=VMEM_LIMIT)

    sizes = [count + (extra if k in (1, bands - 1) else 0) for k in range(bands)]
    packed = pl.pallas_call(
        functools.partial(pack_kernel, bands),
        out_shape=[shape(size, 8, LANES) for size in sizes[1:]] + [shape(4, tiles, EDGE, LANES)] * 2,
        in_specs=[pl.BlockSpec(memory_space=pltpu.HBM)] * 5,
        out_specs=[vmem()] * (bands + 1),
        scratch_shapes=[
            pltpu.VMEM(x.shape, x.dtype) for x in (air_state, fire_level, fuel_left, fuel_class, ignition)
        ]
        + [pltpu.SemaphoreType.DMA((5,))],
        compiler_params=pltpu.CompilerParams(vmem_limit_bytes=PACK_LIMIT),
        name="pack",
    )(air_state, fire_level, fuel_left, fuel_class, ignition)
    slots, up, down = packed[: bands - 1], packed[bands - 1], packed[bands]
    kept = pl.pallas_call(
        functools.partial(keep_kernel, bands),
        out_shape=shape(count, 8, LANES),
        in_specs=[vmem()],
        out_specs=vmem(),
        compiler_params=params,
        cost_estimate=pl.CostEstimate(flops=KEEP_FLOPS, bytes_accessed=0, transcendentals=0),
        name="keep",
    )(air_state)

    rise = [(i, i + 1) for i in range(tile_count - 1)]
    sink = [(j, i) for i, j in rise]

    def turn(values):
        moved = [values[0]]
        for k in range(1, bands):
            moved.append(lax.ppermute(values[k], BANDS, [(i, (i + k) % bands) for i in range(bands)]))
        return moved

    fire_up = lax.ppermute(down, "tile", rise)
    fire_down = lax.ppermute(up, "tile", sink)
    slots = turn([kept, *slots])
    edges = (bands // 2) * count + 4 * (EDGE // 8)
    up, down = pl.pallas_call(
        functools.partial(relay_kernel, bands, rows),
        out_shape=[shape(edges, 8, LANES)] * 2,
        in_specs=[vmem()] * bands,
        out_specs=[vmem()] * 2,
        compiler_params=params,
        cost_estimate=pl.CostEstimate(flops=RELAY_FLOPS, bytes_accessed=0, transcendentals=0),
        name="relay",
    )(*slots)
    edge_up = lax.ppermute(down, "tile", rise)
    edge_down = lax.ppermute(up, "tile", sink)

    span = rows + 2 * EDGE
    values = pl.pallas_call(
        survey_kernel,
        out_shape=[shape(tiles, span, LANES)] * 4,
        in_specs=[smem()] + [vmem()] * 3,
        out_specs=[vmem()] * 4,
        compiler_params=params,
        cost_estimate=pl.CostEstimate(flops=SURVEY_FLOPS, bytes_accessed=0, transcendentals=0),
        name="survey",
    )(tables, fuel_class, fire_up, fire_down)
    fire = pltpu.VMEM((tiles + 1, span + 2 * PAD, LANES), jnp.float32)
    flat = pltpu.VMEM((tiles + 1, span, LANES), jnp.float32)
    side = pltpu.VMEM((span, LANES), jnp.float32)
    atmosphere = pltpu.VMEM((4, (LEVELS + 2) * 24, LANES), jnp.float32)
    results = pl.pallas_call(
        functools.partial(main_kernel, bands),
        out_shape=[shape(rows, width)] * 2 + [shape(2 * depth, 8, LANES)] * bands,
        in_specs=[smem()] + [vmem()] * (3 + bands + 8),
        out_specs=[vmem()] * (2 + bands),
        scratch_shapes=[fire] * 4 + [flat] * 6 + [atmosphere] * 2 + [side] * 4 + [pltpu.VMEM((2, LEVELS, LANES), jnp.float32)],
        compiler_params=params,
        name="window",
    )(
        tables,
        fire_level,
        fuel_left,
        ignition,
        *slots,
        fire_up,
        fire_down,
        edge_up,
        edge_down,
        *values,
    )
    level_out, fuel_out = results[:2]
    slabs = turn(results[2:])
    air_out = pl.pallas_call(
        functools.partial(unpack_kernel, bands),
        out_shape=shape(*air_state.shape),
        in_specs=[vmem()] * bands,
        out_specs=vmem(),
        compiler_params=params,
        name="unpack",
    )(*slabs)
    return (air_out, level_out, fuel_out)


def solution(mesh):
    placed = (
        P(None, ("sect", "sub"), ("group", "tile"), None),
        P(("group", "tile"), ("sect", "sub")),
        P(("group", "tile"), ("sect", "sub")),
        P(("group", "tile"), ("sect", "sub")),
        P(("group", "tile"), ("sect", "sub")),
        P(),
        P(),
        P(),
        P(),
        P(),
    )
    return jax.shard_map(
        local,
        mesh=mesh,
        in_specs=placed,
        out_specs=(
            P(None, ("sect", "sub"), ("group", "tile"), None),
            P(("group", "tile"), ("sect", "sub")),
            P(("group", "tile"), ("sect", "sub")),
        ),
        check_vma=False,
    )
```

```python
import functools
import math

import jax
import jax.numpy as jnp
from jax import lax
from jax.experimental import pallas as pl
from jax.experimental.pallas import tpu as pltpu
from jax.sharding import PartitionSpec as P

LEVELS = 80
REFINE = 10
STEPS = 4
SUBSTEPS = 4
NFUEL = 13

LANES = 128
HALO = STEPS
EDGE = HALO * REFINE
BULK = 32
HALO_ROWS = 4 * BULK + 8
SENT_ROWS = HALO_ROWS + 8
PAD = 8

air_delta = 0.1
diffusion = 0.2
heat_gain = 20.0
vapour_gain = 20.0
lift_gain = 0.3
wind_gain = 0.5
fire_delta = 0.15

BANDS = ("sect", "sub")
UNROLL_LOOKUP = 4
UNROLL_FIRE = 10
UNROLL_AIR = 16
UNROLL_FINAL = 10
KEEP_FLOPS = 10**9
RELAY_FLOPS = 5 * 10**9
SURVEY_FLOPS = 10**9
FIRST_FLOPS = 3 * 10**9
PACK_LIMIT = 62 * 1024 * 1024
VMEM_LIMIT = 32 * 1024 * 1024


def iota(shape, dim):
    return lax.broadcasted_iota(jnp.int32, shape, dim)


def roll(value, shift, axis):
    return pltpu.roll(value, shift, axis)


def unrolled(low, high, step, body, carry):
    def group(i, carry):
        for n in range(step):
            carry = body(low + i * step + n, carry)
        return carry

    groups = -(-(high - low) // step)
    step = -(-(high - low) // groups)
    whole = (high - low) // step
    carry = lax.fori_loop(0, whole, group, carry)
    for i in range(low + whole * step, high):
        carry = body(i, carry)
    return carry


def level_weights(rate, total):
    scale = total / sum(math.exp(-rate * j / LEVELS) for j in range(LEVELS))
    return jnp.exp(iota((LEVELS, LANES), 0).astype(jnp.float32) * (-rate / LEVELS)) * scale


def band_index():
    return lax.axis_index("sect") * lax.axis_size("sub") + lax.axis_index("sub")


def air_tiles(depth):
    return 2 * depth + -(-depth // 3)


def halo_pack(fields, above):
    rows = fields[0].shape[0]
    sub = iota((8, LANES), 0)
    if above:
        bulk = [field[rows - BULK :] for field in fields]
        odd = [fields[a][rows - BULK - 8 : rows - BULK] for a in (0, 2, 3)]
        strip = jnp.where(sub >= 6, odd[0], jnp.where(sub >= 4, roll(odd[1], 6, 0), roll(odd[2], 4, 0)))
    else:
        bulk = [field[:BULK] for field in fields]
        odd = [fields[a][BULK : BULK + 8] for a in (0, 2, 3)]
        strip = jnp.where(sub < 2, odd[0], jnp.where(sub < 4, roll(odd[1], 2, 0), roll(odd[2], 4, 0)))
    return jnp.concatenate(bulk + [strip], axis=0)


def halo_unpack(packed, a, above):
    bulk = packed[a * BULK : (a + 1) * BULK]
    turn = {0: 0, 1: 0, 2: 2, 3: 4}[a]
    strip = packed[4 * BULK : HALO_ROWS]
    if turn:
        strip = roll(strip, turn if above else 8 - turn, 0)
    return jnp.concatenate([strip, bulk] if above else [bulk, strip], axis=0)


def pack_slot(bands, k, air_ref, slot):
    depth = air_ref.shape[1]
    lane_tiles = air_ref.shape[3] // LANES
    lane = iota((8, LANES), 1)
    dest = lax.rem(band_index() + k, bands)
    odd = lax.rem(dest, 2)
    own = pl.multiple_of((dest // 2) * LANES, LANES)
    high = (dest + 1) // 2
    right = pl.multiple_of(jnp.minimum(high, lane_tiles - 1) * LANES, LANES)
    left = pl.multiple_of(jnp.maximum(high - 1, 0) * LANES, LANES)
    turn = 64 * odd
    back = 64 - turn
    from_right = lane < 96 - turn
    for l in range(depth):
        for p in range(2):
            first = air_ref[2 * p, l, :, pl.ds(own, LANES)]
            second = air_ref[2 * p + 1, l, :, pl.ds(own, LANES)]
            slot[2 * l + p] = jnp.where(lane < 64, roll(first, turn, 1), roll(second, back, 1))
    for g in range(-(-depth // 3)):
        packed = jnp.zeros((8, LANES), jnp.float32)
        for l in range(3 * g, min(3 * g + 3, depth)):
            for f in range(4):
                j = (l - 3 * g) * 4 + f
                edge = jnp.where(
                    from_right, air_ref[f, l, :, pl.ds(right, LANES)], air_ref[f, l, :, pl.ds(left, LANES)]
                )
                edge = roll(edge, 4 * j + back, 1)
                here = ((lane >= 4 * j) & (lane < 4 * j + 4)) | ((lane >= 60 + 4 * j) & (lane < 64 + 4 * j))
                packed = jnp.where(here, edge, packed)
        slot[2 * depth + g] = packed


def pack_kernel(bands, *refs):
    sources, targets = refs[:5], refs[5 : bands + 6]
    scratch, outs, sems = refs[bands + 6 : bands + 11], refs[bands + 11 : 2 * bands + 12], refs[2 * bands + 12]
    slots = outs[: bands - 1]
    copies = [pltpu.make_async_copy(a, b, sems.at[n]) for n, (a, b) in enumerate(zip(sources, scratch))]
    for copy in copies:
        copy.start()
    air_ref, level_ref, fuel_ref, class_ref, ignite_ref = scratch
    base = air_tiles(air_ref.shape[1])
    rows, width = level_ref.shape
    sent = []

    def send(n, first=None, count=None):
        source, target = outs[n], targets[n]
        if count is not None:
            source, target = source.at[pl.ds(first, count)], target.at[pl.ds(first, count)]
        sent.append(pltpu.make_async_copy(source, target, sems.at[5 + len(sent)]))
        sent[-1].start()

    copies[0].wait()
    for k in range(1, bands):
        pack_slot(bands, k, air_ref, slots[k - 1])
        send(k - 1, 0, base)
    weights = refs[2 * bands + 13]
    weights[...] = level_weights(1.0, 1.0)
    depth = air_ref.shape[1]
    sub = iota((8, LANES), 0)
    for j in range(width // LANES):
        share = [jnp.zeros((8, LANES), jnp.float32)] * 2
        if j < air_ref.shape[3] // LANES:
            for l in range(depth):
                weight = weights[pl.ds(band_index() * depth + l, 1)]
                for f in range(2):
                    share[f] = share[f] + weight * air_ref[2 + f, l, :, j * LANES : (j + 1) * LANES]
        outs[bands - 1][j, HALO_ROWS:] = jnp.where(sub < 4, share[0], roll(share[1], 4, 0))
        outs[bands][j, HALO_ROWS:] = jnp.where(sub < 4, roll(share[0], 4, 0), share[1])
    for copy in copies[1:]:
        copy.wait()
    fields = [ref[...] for ref in (level_ref, fuel_ref)]
    fields += [ref[...].astype(jnp.float32) for ref in (class_ref, ignite_ref)]
    for n, above in ((bands - 1, False), (bands, True)):
        for j in range(width // LANES):
            outs[n][j, :HALO_ROWS] = halo_pack([field[:, j * LANES : (j + 1) * LANES] for field in fields], above)
        send(n)
    wide = iota((rows, LANES), 1)
    for pair in range(2):
        first, second = fields[2 * pair], fields[2 * pair + 1]
        at = pl.ds(base + pair * (rows // 8), rows // 8)
        to_next = jnp.where(wide < 64, roll(second[:, width - LANES :], 64, 1), first[:, width - LANES :])
        slots[0][at] = to_next.reshape(rows // 8, 8, LANES)
        to_prev = jnp.where(wide < 64, first[:, :LANES], roll(second[:, :LANES], 64, 1))
        slots[bands - 2][at] = to_prev.reshape(rows // 8, 8, LANES)
    send(0, base, 2 * (rows // 8))
    send(bands - 2, base, 2 * (rows // 8))
    for copy in sent:
        copy.wait()


def keep_kernel(bands, air_ref, slot):
    pack_slot(bands, 0, air_ref, slot)


def corner_tiles(next_ref, prev_ref, base, rows):
    lane = iota((rows, LANES), 1)
    result = []
    for pair in range(2):
        at = pl.ds(base + pair * (rows // 8), rows // 8)
        left = prev_ref[at].reshape(rows, LANES)
        right = next_ref[at].reshape(rows, LANES)
        result.append(jnp.where(lane < 64, right, left))
        result.append(roll(jnp.where(lane < 64, left, right), 64, 1))
    return result


def relay_kernel(bands, rows, *refs):
    slots, (up_ref, down_ref, wind_ref, weights) = refs[:bands], refs[bands:]
    tiles = slots[0].shape[0]
    depth = LEVELS // bands
    lane = iota((8, LANES), 1)
    sub = iota((8, LANES), 0)
    for half in range(bands // 2):
        one, two = slots[2 * half], slots[2 * half + 1]

        def body(i, carry, one=one, two=two, half=half):
            first, second = one[i], two[i]
            up_ref[half * tiles + i] = jnp.where(sub < 4, first, roll(second, 4, 0))
            down_ref[half * tiles + i] = jnp.where(sub < 4, roll(first, 4, 0), second)
            return carry

        unrolled(0, tiles, 8, body, 0)

    weights[...] = level_weights(1.0, 1.0)
    inner = [jnp.zeros((8, LANES), jnp.float32)] * 2
    edges = jnp.zeros((8, LANES), jnp.float32)
    for k in range(bands):
        first = lax.rem(band_index() - k + bands, bands) * depth
        for l in range(depth):
            inner[l % 2] = inner[l % 2] + weights[pl.ds(first + l, 1)] * slots[k][2 * l + 1]
        for g in range(-(-depth // 3)):
            parts = [weights[pl.ds(first + min(3 * g + n, depth - 1), 1)] for n in range(3)]
            weight = jnp.where(
                (lane < 16) | ((lane >= 60) & (lane < 76)),
                parts[0],
                jnp.where((lane < 32) | ((lane >= 76) & (lane < 92)), parts[1], parts[2]),
            )
            edges = edges + weight * slots[k][2 * depth + g]
    inner = inner[0] + inner[1]
    for f in range(2):
        halo = sum(roll(edges, 64 - 4 * (4 * n + 2 + f), 1) for n in range(3))
        wind_ref[f] = jnp.where(lane < 64, inner if f == 0 else roll(inner, 64, 1), halo)


def corner_kernel(bands, lane_tiles, up_ref, down_ref, *outs):
    tiles = up_ref.shape[0]
    lane = iota((8, LANES), 1)
    wide = iota((HALO_ROWS, LANES), 1)
    for k in range(bands):
        dest = lax.rem(band_index() + k, bands)
        odd = lax.rem(dest, 2)
        high = (dest + 1) // 2
        right = jnp.minimum(high, lane_tiles - 1)
        left = jnp.maximum(high - 1, 0)
        turn = 64 * odd
        for n, ref in enumerate((up_ref, down_ref)):
            inner, after, before = (ref[j, HALO_ROWS:] for j in (dest // 2, right, left))
            edge = jnp.where(lane < 96 - turn, after, before)
            outs[k][n] = jnp.where(lane < 64, roll(inner, turn, 1), roll(edge, turn, 1))
    at = pl.ds(2, HALO_ROWS // 8)
    up, down = up_ref[tiles - 1, :HALO_ROWS], down_ref[tiles - 1, :HALO_ROWS]
    outs[1][at] = jnp.where(wide < 64, roll(down, 64, 1), up).reshape(HALO_ROWS // 8, 8, LANES)
    up, down = up_ref[0, :HALO_ROWS], down_ref[0, :HALO_ROWS]
    outs[bands - 1][at] = jnp.where(wide < 64, up, roll(down, 64, 1)).reshape(HALO_ROWS // 8, 8, LANES)


def table_vectors(tables_ref):
    lane = iota((8, LANES), 1)
    vectors = []
    for n in range(4):
        vector = jnp.zeros((8, LANES), jnp.float32)
        for category in range(NFUEL):
            vector = jnp.where(lane == category, tables_ref[n, category], vector)
        vectors.append(vector)
    vectors[1] = -1.0 / jnp.where(lane < NFUEL, vectors[1], 1.0)
    return vectors


def pick(vector, index):
    return jnp.take_along_axis(vector, index, axis=1, mode="promise_in_bounds")


def survey_kernel(tables_ref, class_ref, up_ref, down_ref, *outs):
    vectors = table_vectors(tables_ref)
    rows, width = class_ref.shape
    tiles = width // LANES

    def put(j, at, classes):
        index = classes.astype(jnp.int32)
        for vector, out in zip(vectors, outs):
            out[j, at] = pick(vector, index)

    for j in range(tiles):
        for first, ref, above in ((0, up_ref, True), (EDGE + rows, down_ref, False)):
            classes = halo_unpack(ref[j], 2, above)
            for n in range(0, EDGE, 8):
                put(j, slice(first + n, first + n + 8), classes[n : n + 8])

    def body(t, carry):
        for j in range(tiles):
            at = pl.ds(pl.multiple_of(EDGE + 8 * t, 8), 8)
            put(j, at, class_ref[pl.ds(pl.multiple_of(8 * t, 8), 8), j * LANES : (j + 1) * LANES])
        return carry

    unrolled(0, rows // 8, 5, body, 0)


def slab_masks(bands):
    tile, band, tile_count = lax.axis_index("tile"), band_index(), lax.axis_size("tile")
    first_tile, final_tile = tile == 0, tile == tile_count - 1
    first_band, final_band = band == 0, band == bands - 1
    lane, sub = iota((8, LANES), 1), iota((8, LANES), 0)
    low_row = jnp.where(final_tile, 0, 4)
    high_row = jnp.where(first_tile, 8, 4)
    low_lane = jnp.where(final_band, 64, 68)
    high_lane = jnp.where(first_band, 128, 124)
    inside_own = (lane < low_lane) | (lane >= high_lane)
    inside = (inside_own, inside_own & ((sub < low_row) | (sub >= high_row)))
    return first_tile, final_tile, first_band, final_band, inside


def swap(a, b):
    sub = iota((8, LANES), 0)
    a, b = roll(a, 4, 0), roll(b, 4, 0)
    return jnp.where(sub < 4, a, b), jnp.where(sub < 4, b, a)


def strip(t, base=PAD):
    return pl.ds(pl.multiple_of(base + 8 * t, 8), 8)


def fire_steps(bands, tables_ref, tiles, rows, ignite, values_in, values_side, scratch):
    pace, burnt, wind_u, wind_v, energy, vapour = scratch
    first_tile, final_tile, first_band, final_band, inside = slab_masks(bands)
    own = PAD + EDGE
    span = rows + 2 * EDGE
    lane = iota((8, LANES), 1)
    for held in (energy, vapour):
        for j in range(tiles + 1):
            held[j, :16] = jnp.zeros((16, LANES), jnp.float32)
            held[j, span - 16 :] = jnp.zeros((16, LANES), jnp.float32)

    def value_at(n, j, t):
        return values_in[n][j, strip(t, 0)] if j < tiles else values_side[n][strip(t, 0)]

    def kindled(values, t, c):
        return [
            jnp.where(ignite[j, strip(t)] <= c, jnp.minimum(value, -1.0), value) for j, value in enumerate(values)
        ]

    mend_low = first_band & (lane == LANES - 1)
    mend_high = final_band & (lane == 0)

    def mend_lanes(values):
        halo = jnp.where(mend_low, roll(values[0], LANES - 1, 1), values[tiles])
        halo = jnp.where(mend_high, roll(values[tiles - 1], 1, 1), halo)
        return values[:tiles] + [halo]

    def mend_rows(held):
        @pl.when(first_tile)
        def _():
            for j in range(tiles + 1):
                held[j, own - 1 : own] = held[j, own : own + 1]

        @pl.when(final_tile)
        def _():
            for j in range(tiles + 1):
                held[j, own + rows : own + rows + 1] = held[j, own + rows - 1 : own + rows]

    def covers(shape, cell_dim):
        cell, column = iota(shape, cell_dim), iota(shape, 1 - cell_dim)
        start = jnp.where(
            column < 64 + HALO,
            REFINE * column,
            jnp.where(column >= LANES - HALO, REFINE * column + (tiles + 1 - REFINE) * LANES, -LANES * 1000),
        )
        return jnp.where((cell >= start) & (cell < start + REFINE), 1.0, 0.0).astype(jnp.bfloat16)

    cells = (tiles + 1) * LANES
    to_cells = jnp.concatenate([covers((LANES, cells), 1)] * 2, axis=0)
    to_columns = jnp.concatenate([covers((cells, LANES), 0)] * 2, axis=0)

    def parts(value, axis):
        high = value.astype(jnp.bfloat16)
        low = (value - high.astype(jnp.float32)).astype(jnp.bfloat16)
        return jnp.concatenate([high, low], axis=axis)

    def dot(a, b):
        return jnp.dot(a, b, preferred_element_type=jnp.float32)

    def couple(c, wind, chain, fuel_from, fuel_to):
        reach = EDGE - REFINE * (c + 1)
        fire_step = tables_ref[4, c]

        def strips(margin):
            return (EDGE - margin) // 8, -(-(EDGE + rows + margin) // 8)

        coarse = [half for n in range(2) for half in swap(wind[2 * n + 1], wind[2 * n])]
        wide = dot(parts(jnp.concatenate(coarse, axis=0) * wind_gain, 1), to_cells)
        for n, held in enumerate((wind_u, wind_v)):
            for j in range(tiles + 1):
                for half in range(2):
                    value = wide[16 * n + 8 * half : 16 * n + 8 * half + 8, j * LANES : (j + 1) * LANES]
                    for row in range(REFINE):
                        held[j, pl.ds(half * (span // 2) + row, 8, stride=REFINE)] = value

        for s in range(SUBSTEPS):
            before, after = chain[s], chain[s + 1]

            def advance(t, carry, c=c, s=s, fire_step=fire_step, before=before, after=after):
                row = pl.multiple_of(PAD + 8 * t, 8)
                at, flat = strip(t), strip(t, 0)
                centre = [before[j, at] for j in range(tiles + 1)]
                lower = [roll(value, 1, 1) for value in centre]
                upper = [roll(value, LANES - 1, 1) for value in centre]
                result = []
                for j in range(tiles + 1):
                    west = before[j, pl.ds(row - 1, 8)]
                    east = before[j, pl.ds(row + 1, 8)]
                    south = jnp.where(lane == 0, lower[j - 1], lower[j])
                    north = jnp.where(lane == LANES - 1, upper[(j + 1) % (tiles + 1)], upper[j])
                    here = centre[j]
                    back, ahead = here - west, east - here
                    below, above = here - south, north - here
                    a, b = jnp.maximum(back, 0.0), jnp.minimum(ahead, 0.0)
                    d, e = jnp.maximum(below, 0.0), jnp.minimum(above, 0.0)
                    square = (a * a + b * b) + (d * d + e * e)
                    steep = square * lax.rsqrt(jnp.maximum(square, 1.2e-38))
                    gx, gy = back + ahead, below + above
                    tail = (wind_u[j, flat] * gx + wind_v[j, flat] * gy) * lax.rsqrt((gx * gx + 4.0) + gy * gy)
                    if s == 0:
                        speed = fire_step * value_at(0, j, t)
                        pace[j, flat] = speed
                    else:
                        speed = pace[j, flat]
                    result.append(here - (speed * (1.0 + jnp.maximum(tail, 0.0))) * steep)
                for j in range(tiles + 1):
                    unburnt = jnp.clip(result[j], -0.5, 0.5)
                    if s > 0:
                        unburnt = unburnt + burnt[j, flat]
                    if s < SUBSTEPS - 1:
                        burnt[j, flat] = unburnt
                    else:
                        held = fuel_from[j, at]
                        remain = held * jnp.exp((0.5 * SUBSTEPS - unburnt) * (fire_step * value_at(1, j, t)))
                        spent = held - remain
                        fuel_to[j, at] = remain
                        energy[j, flat] = spent * value_at(2, j, t)
                        vapour[j, flat] = spent * value_at(3, j, t)
                if s == SUBSTEPS - 1 and c < STEPS - 1:
                    result = kindled(result, t, c + 1)
                for j, value in enumerate(mend_lanes(result)):
                    after[j, at] = value
                return carry

            unrolled(*strips(reach + SUBSTEPS - 1 - s), UNROLL_FIRE, advance, 0)
            mend_rows(after)

        totals = []
        for held in (energy, vapour):
            for half in range(2):
                total = []
                for j in range(tiles + 1):
                    value = [held[j, pl.ds(half * (span // 2) + row, 8, stride=REFINE)] for row in range(REFINE)]
                    while len(value) > 1:
                        value = [sum(value[n : n + 2]) for n in range(0, len(value), 2)]
                    total.append(value[0])
                totals.append(jnp.concatenate(total, axis=1))
        flux = dot(parts(jnp.concatenate(totals, axis=0), 1), to_columns)
        forcing = []
        for n, gain in enumerate((heat_gain, vapour_gain)):
            first, second = (flux[16 * n + 8 * half : 16 * n + 8 * half + 8] for half in range(2))
            halo, inner = swap(second, first)
            scale = air_delta * gain / (REFINE * REFINE)
            forcing.append([jnp.where(mask, value * scale, 0.0) for mask, value in zip(inside, (inner, halo))])
        return forcing

    return couple, kindled, mend_lanes, mend_rows


def first_kernel(bands, tables_ref, level_in, fuel_in, ignite_in, next_ref, prev_ref, wind_own, *refs):
    fire_up, fire_down = refs[:2]
    sides, refs = refs[2 : bands + 2], refs[bands + 2 :]
    values_in = refs[:4]
    level_out, fuel, ignite, flux_out = refs[4:8]
    values_side = refs[8:12]
    lev_a, lev_b = refs[12:14]
    scratch = refs[14:]
    rows, width = level_in.shape
    tiles = width // LANES
    own = PAD + EDGE
    span = rows + 2 * EDGE
    sub = iota((8, LANES), 0)

    corners = corner_tiles(next_ref, prev_ref, air_tiles(LEVELS // bands), rows)
    at = pl.ds(2, HALO_ROWS // 8)
    left, right = (ref[at].reshape(HALO_ROWS, LANES) for ref in (sides[1], sides[bands - 1]))
    wide = iota((HALO_ROWS, LANES), 1)
    upper_side = jnp.where(wide < 64, right, left)
    lower_side = roll(jnp.where(wide < 64, left, right), 64, 1)
    for a, (source, held) in enumerate(((level_in, lev_a), (fuel_in, fuel), (None, None), (ignite_in, ignite))):
        upper, lower = halo_unpack(upper_side, a, True), halo_unpack(lower_side, a, False)
        if held is None:
            side = jnp.concatenate([upper, corners[a], lower], axis=0).astype(jnp.int32)
            vectors = table_vectors(tables_ref)
            for n in range(span // 8):
                for vector, out in zip(vectors, values_side):
                    out[8 * n : 8 * n + 8] = pick(vector, side[8 * n : 8 * n + 8])
            continue
        for j in range(tiles):
            held[j, PAD:own] = halo_unpack(fire_up[j], a, True)
            held[j, own : own + rows] = source[:, j * LANES : (j + 1) * LANES].astype(jnp.float32)
            held[j, own + rows : own + rows + EDGE] = halo_unpack(fire_down[j], a, False)
        held[tiles, PAD:own] = upper
        held[tiles, own : own + rows] = corners[a]
        held[tiles, own + rows : own + rows + EDGE] = lower
    spare = jnp.zeros((tiles + 1, PAD, LANES), jnp.float32)
    for held in (lev_a, lev_b):
        held[:, :PAD] = spare
        held[:, PAD + span :] = spare

    couple, kindled, mend_lanes, mend_rows = fire_steps(
        bands, tables_ref, tiles, rows, ignite, values_in, values_side, scratch
    )

    def kindle(t, carry):
        values = mend_lanes(kindled([lev_a[j, strip(t)] for j in range(tiles + 1)], t, 0))
        for j, value in enumerate(values):
            lev_a[j, strip(t)] = value
        return carry

    unrolled(0, span // 8, UNROLL_LOOKUP, kindle, 0)
    mend_rows(lev_a)


    inside = slab_masks(bands)[4]
    above, below = (sum(ref[n] for ref in sides) for n in range(2))
    halo_u = jnp.where(sub < 4, below, roll(above, 4, 0))
    halo_v = jnp.where(sub < 4, roll(below, 4, 0), above)
    wind = []
    for value, halo in ((wind_own[0], halo_u), (wind_own[1], halo_v)):
        wind += [jnp.where(inside[0], value, 0.0), jnp.where(inside[1], halo, 0.0)]
    forcing = couple(0, wind, (lev_a, lev_b, lev_a, lev_b, level_out), fuel, fuel)
    for n in range(2):
        for part in range(2):
            flux_out[2 * n + part] = forcing[n][part]


def main_kernel(bands, tables_ref, level_in, fuel_in, ignite, flux_in, *refs):
    slots = refs[:bands]
    edge_up, edge_down = refs[bands : bands + 2]
    values_in = refs[bands + 2 : bands + 6]
    values_side = refs[bands + 6 : bands + 10]
    level_out, fuel_out = refs[bands + 10 : bands + 12]
    outs = refs[bands + 12 : 2 * bands + 12]
    scratch = refs[2 * bands + 12 :]
    lev_a, lev_b, fuel = scratch[:3]
    air_a, air_b, weights = scratch[9:12]
    rows, width = level_out.shape
    tiles = width // LANES
    depth = LEVELS // bands
    count = air_tiles(depth)
    own = PAD + EDGE
    lane = iota((8, LANES), 1)
    band = band_index()
    couple = fire_steps(bands, tables_ref, tiles, rows, ignite, values_in, values_side, scratch[3:9])[0]

    sub = iota((8, LANES), 0)
    inside = slab_masks(bands)[4]

    def layer_at(k, part, shift=0):
        return pl.ds(pl.multiple_of((k + 1) * 24 + 8 * part, 8) + shift, 8)

    def put(held, f, k, part, value):
        held[f, layer_at(k, part)] = value
        if part == 2:
            held[f, layer_at(k, 0)] = value

    for k in range(bands):
        source = lax.rem(band - k + bands, bands)
        half = k // 2

        def whole(i, k=k, half=half):
            below, above = edge_down[half * count + i], edge_up[half * count + i]
            if k % 2 == 0:
                halo = jnp.where(sub < 4, below, roll(above, 4, 0))
            else:
                halo = jnp.where(sub < 4, roll(below, 4, 0), above)
            return slots[k][i], halo

        for g in range(-(-depth // 3)):
            edges = whole(2 * depth + g)
            for l in range(3 * g, min(3 * g + 3, depth)):
                for p in range(2):
                    both = whole(2 * l + p)
                    for f in range(2):
                        j = (l - 3 * g) * 4 + 2 * p + f
                        for part in range(2):
                            inner = both[part] if f == 0 else roll(both[part], 64, 1)
                            value = jnp.where(lane < 64, inner, roll(edges[part], 64 - 4 * j, 1))
                            value = jnp.where(inside[part], value, 0.0)
                            put(air_a, 2 * p + f, source * depth + l, part + 1, value)
    nothing = jnp.zeros((8, LANES), jnp.float32)
    for held in (air_a, air_b):
        for f in range(4):
            for part in range(3):
                held[f, layer_at(-1, part)] = nothing
                held[f, layer_at(LEVELS, part)] = nothing

    weights[0] = level_weights(2.0, float(LEVELS))
    weights[1] = level_weights(1.0, 1.0)
    def blow(total, k, result):
        weight = weights[1, pl.ds(k, 1)]
        return [a + weight * b for a, b in zip(total, result)]

    calm = [nothing] * 4
    spread = air_delta * diffusion
    mixing = [jnp.where(mask, spread, 0.0) for mask in inside]
    lifting = [jnp.where(mask, 0.5 * lift_gain * air_delta, 0.0) for mask in inside]
    lifting = [(value, 0.6 * value) for value in lifting]
    state, other = air_a, air_b
    for c in range(STEPS):
        if c == 0:
            forcing = [[flux_in[2 * n + part] for part in range(2)] for n in range(2)]
        else:
            chain = (level_in if c == 1 else lev_a, lev_b, lev_a, lev_b, lev_a)
            forcing = couple(c, wind, chain, fuel_in if c == 1 else fuel, fuel)

        def air_step(k, part, height, state=state, forcing=forcing):
            at = layer_at(k, part + 1)
            here = [state[f, at] for f in range(4)]
            west = [state[f, layer_at(k, part + 1, -1)] for f in range(4)]
            east = [state[f, layer_at(k, 1 if part == 0 else 0, 1)] for f in range(4)]
            south = [roll(value, 1, 1) for value in here]
            north = [roll(value, LANES - 1, 1) for value in here]
            u, v = air_delta * here[2], air_delta * here[3]
            mix = mixing[part]
            to_west, to_east = mix + jnp.maximum(u, 0.0), mix - jnp.minimum(u, 0.0)
            to_south, to_north = mix + jnp.maximum(v, 0.0), mix - jnp.minimum(v, 0.0)
            keep = (1.0 - 6.0 * spread) - (jnp.abs(u) + jnp.abs(v))
            result = []
            for f in range(4):
                new = keep * here[f] + mix * (state[f, layer_at(k - 1, part + 1)] + state[f, layer_at(k + 1, part + 1)])
                new = new + (to_west * west[f] + to_east * east[f]) + (to_south * south[f] + to_north * north[f])
                if f < 2:
                    new = new + height * forcing[f][part]
                else:
                    low, high = (west, east) if f == 2 else (south, north)
                    new = new + (lifting[part][0] * (high[0] - low[0]) + lifting[part][1] * (high[1] - low[1]))
                result.append(new)
            return result

        if c < STEPS - 1:

            def layer(k, carry, other=other, air_step=air_step):
                height = weights[0, pl.ds(k, 1)]
                result = [air_step(k, part, height) for part in range(2)]
                for part in range(2):
                    for f in range(4):
                        put(other, f, k, part + 1, result[part][f])
                return blow(carry, k, [result[part][f] for f in (2, 3) for part in range(2)])

            wind = unrolled(0, LEVELS, UNROLL_AIR, layer, calm)
            state, other = other, state
        else:
            for k in range(bands):
                first = lax.rem(band + k, bands) * depth

                def final(l, carry, out=outs[k], first=first, air_step=air_step):
                    result = air_step(first + l, 0, weights[0, pl.ds(first + l, 1)])
                    for p in range(2):
                        out[2 * l + p] = jnp.where(lane < 64, result[2 * p], roll(result[2 * p + 1], 64, 1))
                    return carry

                unrolled(0, depth, UNROLL_FINAL, final, 0)

    for j in range(tiles):
        level_out[:, j * LANES : (j + 1) * LANES] = lev_a[j, own : own + rows]
        fuel_out[:, j * LANES : (j + 1) * LANES] = fuel[j, own : own + rows]


def unpack_kernel(bands, *refs):
    slots, out = refs[:bands], refs[bands]
    depth = out.shape[1]
    lane = iota((8, LANES), 1)
    for k in range(bands):
        source = lax.rem(band_index() - k + bands, bands)
        odd = lax.rem(source, 2)
        cols = pl.ds(pl.multiple_of((source // 2) * LANES, LANES), LANES)
        mine = (lane >= 64 * odd) & (lane < 64 * odd + 64)

        def body(l, carry, slot=slots[k], odd=odd, cols=cols, mine=mine):
            for p in range(2):
                both = slot[2 * l + p]
                for f in range(2):
                    shift = 64 * odd if f == 0 else 64 - 64 * odd
                    old = out[2 * p + f, l, :, cols]
                    out[2 * p + f, l, :, cols] = jnp.where(mine, roll(both, shift, 1), old)
            return carry

        unrolled(0, depth, 10, body, 0)


def shape(*dims):
    return jax.ShapeDtypeStruct(dims, jnp.float32)


def vmem():
    return pl.BlockSpec(memory_space=pltpu.VMEM)


def smem():
    return pl.BlockSpec(memory_space=pltpu.SMEM)


def local(
    air_state,
    fire_level,
    fuel_left,
    fuel_class,
    ignition,
    plan,
    spread_rate,
    burn_time,
    heat_content,
    moisture_content,
):
    steps = jnp.pad(plan.astype(jnp.float32) * fire_delta, (0, NFUEL - STEPS))
    tables = jnp.stack([spread_rate, burn_time, heat_content, moisture_content, steps])
    bands = lax.axis_size(BANDS)
    tile_count = lax.axis_size("tile")
    depth = air_state.shape[1]
    rows, width = fire_level.shape
    tiles = width // LANES
    count = air_tiles(depth)
    extra = 2 * (rows // 8)
    params = pltpu.CompilerParams(vmem_limit_bytes=VMEM_LIMIT)

    sizes = [count + (extra if k in (1, bands - 1) else 0) for k in range(bands)]
    packed = pl.pallas_call(
        functools.partial(pack_kernel, bands),
        out_shape=[shape(size, 8, LANES) for size in sizes[1:]] + [shape(tiles, SENT_ROWS, LANES)] * 2,
        in_specs=[pl.BlockSpec(memory_space=pltpu.HBM)] * 5,
        out_specs=[pl.BlockSpec(memory_space=pltpu.HBM)] * (bands + 1),
        scratch_shapes=[
            pltpu.VMEM(x.shape, x.dtype) for x in (air_state, fire_level, fuel_left, fuel_class, ignition)
        ]
        + [pltpu.VMEM((size, 8, LANES), jnp.float32) for size in sizes[1:]]
        + [pltpu.VMEM((tiles, SENT_ROWS, LANES), jnp.float32)] * 2
        + [pltpu.SemaphoreType.DMA((bands + 8,)), pltpu.VMEM((LEVELS, LANES), jnp.float32)],
        compiler_params=pltpu.CompilerParams(vmem_limit_bytes=PACK_LIMIT),
        name="pack",
    )(air_state, fire_level, fuel_left, fuel_class, ignition)
    slots, up, down = packed[: bands - 1], packed[bands - 1], packed[bands]
    kept = pl.pallas_call(
        functools.partial(keep_kernel, bands),
        out_shape=shape(count, 8, LANES),
        in_specs=[vmem()],
        out_specs=vmem(),
        compiler_params=params,
        cost_estimate=pl.CostEstimate(flops=KEEP_FLOPS, bytes_accessed=0, transcendentals=0),
        name="keep",
    )(air_state)

    rise = [(i, i + 1) for i in range(tile_count - 1)]
    sink = [(j, i) for i, j in rise]

    def turn(values):
        moved = [values[0]]
        for k in range(1, bands):
            moved.append(lax.ppermute(values[k], BANDS, [(i, (i + k) % bands) for i in range(bands)]))
        return moved

    fire_up = lax.ppermute(down, "tile", rise)
    fire_down = lax.ppermute(up, "tile", sink)
    slots = turn([kept, *slots])
    edges = (bands // 2) * count
    up, down, wind = pl.pallas_call(
        functools.partial(relay_kernel, bands, rows),
        out_shape=[shape(edges, 8, LANES)] * 2 + [shape(2, 8, LANES)],
        in_specs=[vmem()] * bands,
        out_specs=[vmem()] * 3,
        scratch_shapes=[pltpu.VMEM((LEVELS, LANES), jnp.float32)],
        compiler_params=params,
        cost_estimate=pl.CostEstimate(flops=RELAY_FLOPS, bytes_accessed=0, transcendentals=0),
        name="relay",
    )(*slots)
    edge_up = lax.ppermute(down, "tile", rise)
    edge_down = lax.ppermute(up, "tile", sink)
    sides = pl.pallas_call(
        functools.partial(corner_kernel, bands, air_state.shape[3] // LANES),
        out_shape=[
            shape(2 + (HALO_ROWS // 8 if k in (1, bands - 1) else 0), 8, LANES) for k in range(bands)
        ],
        in_specs=[vmem()] * 2,
        out_specs=[vmem()] * bands,
        compiler_params=params,
        name="corners",
    )(fire_up, fire_down)
    sides = turn(sides)

    span = rows + 2 * EDGE
    values = pl.pallas_call(
        survey_kernel,
        out_shape=[shape(tiles, span, LANES)] * 4,
        in_specs=[smem()] + [vmem()] * 3,
        out_specs=[vmem()] * 4,
        compiler_params=params,
        cost_estimate=pl.CostEstimate(flops=SURVEY_FLOPS, bytes_accessed=0, transcendentals=0),
        name="survey",
    )(tables, fuel_class, fire_up, fire_down)
    padded = (tiles + 1, span + 2 * PAD, LANES)
    fire = pltpu.VMEM(padded, jnp.float32)
    flat = pltpu.VMEM((tiles + 1, span, LANES), jnp.float32)
    atmosphere = pltpu.VMEM((4, (LEVELS + 2) * 24, LANES), jnp.float32)
    level, fuel, ignite, flux, *values_side = pl.pallas_call(
        functools.partial(first_kernel, bands),
        out_shape=[shape(*padded)] * 3 + [shape(4, 8, LANES)] + [shape(span, LANES)] * 4,
        in_specs=[smem()] + [vmem()] * (12 + bands),
        out_specs=[vmem()] * 8,
        scratch_shapes=[fire] * 2 + [flat] * 6,
        compiler_params=params,
        cost_estimate=pl.CostEstimate(flops=FIRST_FLOPS, bytes_accessed=0, transcendentals=0),
        name="first",
    )(
        tables,
        fire_level,
        fuel_left,
        ignition,
        slots[bands - 1],
        slots[1],
        wind,
        fire_up,
        fire_down,
        *sides,
        *values,
    )
    results = pl.pallas_call(
        functools.partial(main_kernel, bands),
        out_shape=[shape(rows, width)] * 2 + [shape(2 * depth, 8, LANES)] * bands,
        in_specs=[smem()] + [vmem()] * (4 + bands + 10),
        out_specs=[vmem()] * (2 + bands),
        scratch_shapes=[fire] * 3 + [flat] * 6 + [atmosphere] * 2 + [pltpu.VMEM((2, LEVELS, LANES), jnp.float32)],
        compiler_params=params,
        name="window",
    )(
        tables,
        level,
        fuel,
        ignite,
        flux,
        *slots,
        edge_up,
        edge_down,
        *values,
        *values_side,
    )
    level_out, fuel_out = results[:2]
    slabs = turn(results[2:])
    air_out = pl.pallas_call(
        functools.partial(unpack_kernel, bands),
        out_shape=shape(*air_state.shape),
        in_specs=[vmem()] * bands,
        out_specs=vmem(),
        compiler_params=params,
        name="unpack",
    )(*slabs)
    return (air_out, level_out, fuel_out)


def solution(mesh):
    placed = (
        P(None, ("sect", "sub"), ("group", "tile"), None),
        P(("group", "tile"), ("sect", "sub")),
        P(("group", "tile"), ("sect", "sub")),
        P(("group", "tile"), ("sect", "sub")),
        P(("group", "tile"), ("sect", "sub")),
        P(),
        P(),
        P(),
        P(),
        P(),
    )
    return jax.shard_map(
        local,
        mesh=mesh,
        in_specs=placed,
        out_specs=(
            P(None, ("sect", "sub"), ("group", "tile"), None),
            P(("group", "tile"), ("sect", "sub")),
            P(("group", "tile"), ("sect", "sub")),
        ),
        check_vma=False,
    )
```

```python
import functools
import math

import jax
import jax.numpy as jnp
from jax import lax
from jax.experimental import pallas as pl
from jax.experimental.pallas import tpu as pltpu
from jax.sharding import PartitionSpec as P

LEVELS = 80
REFINE = 10
STEPS = 4
SUBSTEPS = 4
NFUEL = 13

LANES = 128
vapour_lift = 0.6
HALO = STEPS
EDGE = HALO * REFINE
BULK = 32
HALO_ROWS = 4 * BULK + 8
SENT_ROWS = HALO_ROWS + 8
PAD = 8

air_delta = 0.1
diffusion = 0.2
heat_gain = 20.0
vapour_gain = 20.0
lift_gain = 0.3
wind_gain = 0.5
fire_delta = 0.15

BANDS = ("sect", "sub")
UNROLL_LOOKUP = 4
UNROLL_FIRE = 10
UNROLL_AIR = 16
UNROLL_FINAL = 10
KEEP_FLOPS = 10**9
UNPACK_FLOPS = 10**9
RELAY_FLOPS = 5 * 10**9
SURVEY_FLOPS = 10**9
FIRST_FLOPS = 3 * 10**9
PACK_LIMIT = 62 * 1024 * 1024
VMEM_LIMIT = 32 * 1024 * 1024


def iota(shape, dim):
    return lax.broadcasted_iota(jnp.int32, shape, dim)


def roll(value, shift, axis):
    return pltpu.roll(value, shift, axis)


def unrolled(low, high, step, body, carry):
    def group(i, carry):
        for n in range(step):
            carry = body(low + i * step + n, carry)
        return carry

    groups = -(-(high - low) // step)
    step = -(-(high - low) // groups)
    whole = (high - low) // step
    carry = lax.fori_loop(0, whole, group, carry)
    for i in range(low + whole * step, high):
        carry = body(i, carry)
    return carry


def level_weights(rate, total):
    scale = total / sum(math.exp(-rate * j / LEVELS) for j in range(LEVELS))
    return jnp.exp(iota((LEVELS, LANES), 0).astype(jnp.float32) * (-rate / LEVELS)) * scale


def band_index():
    return lax.axis_index("sect") * lax.axis_size("sub") + lax.axis_index("sub")


def air_tiles(depth):
    return 2 * depth + -(-depth // 4)


def halo_pack(fields, above):
    rows = fields[0].shape[0]
    sub = iota((8, LANES), 0)
    if above:
        bulk = [field[rows - BULK :] for field in fields]
        odd = [fields[a][rows - BULK - 8 : rows - BULK] for a in (0, 2, 3)]
        strip = jnp.where(sub >= 6, odd[0], jnp.where(sub >= 4, roll(odd[1], 6, 0), roll(odd[2], 4, 0)))
    else:
        bulk = [field[:BULK] for field in fields]
        odd = [fields[a][BULK : BULK + 8] for a in (0, 2, 3)]
        strip = jnp.where(sub < 2, odd[0], jnp.where(sub < 4, roll(odd[1], 2, 0), roll(odd[2], 4, 0)))
    return jnp.concatenate(bulk + [strip], axis=0)


def halo_unpack(packed, a, above):
    bulk = packed[a * BULK : (a + 1) * BULK]
    turn = {0: 0, 1: 0, 2: 2, 3: 4}[a]
    strip = packed[4 * BULK : HALO_ROWS]
    if turn:
        strip = roll(strip, turn if above else 8 - turn, 0)
    return jnp.concatenate([strip, bulk] if above else [bulk, strip], axis=0)


def pack_slot(bands, k, air_ref, slot):
    depth = air_ref.shape[1]
    lane_tiles = air_ref.shape[3] // LANES
    lane = iota((8, LANES), 1)
    dest = lax.rem(band_index() + k, bands)
    odd = lax.rem(dest, 2)
    own = pl.multiple_of((dest // 2) * LANES, LANES)
    high = (dest + 1) // 2
    right = pl.multiple_of(jnp.minimum(high, lane_tiles - 1) * LANES, LANES)
    left = pl.multiple_of(jnp.maximum(high - 1, 0) * LANES, LANES)
    turn = 64 * odd
    back = 64 - turn
    from_right = lane < 96 - turn
    is_odd = jnp.full((8, LANES), odd, jnp.int32) == 1
    for l in range(depth):
        for p in range(2):
            first = air_ref[2 * p, l, :, pl.ds(own, LANES)]
            second = air_ref[2 * p + 1, l, :, pl.ds(own, LANES)]
            turned = roll(jnp.where(is_odd, first, second), 64, 1)
            slot[2 * l + p] = jnp.where(
                lane < 64, jnp.where(is_odd, turned, first), jnp.where(is_odd, second, turned)
            )
    for g in range(-(-depth // 4)):
        packed = jnp.zeros((8, LANES), jnp.float32)
        for l in range(4 * g, min(4 * g + 4, depth)):
            for f in range(4):
                q = (l - 4 * g) * 2 + f // 2
                at = (8 * q + 64 * (f % 2)) % LANES
                edge = jnp.where(
                    from_right, air_ref[f, l, :, pl.ds(right, LANES)], air_ref[f, l, :, pl.ds(left, LANES)]
                )
                edge = roll(edge, lax.rem(at + back, LANES), 1)
                other = (at + 60) % LANES
                here = ((lane >= at) & (lane < at + 4)) | ((lane >= other) & (lane < other + 4))
                packed = jnp.where(here, edge, packed)
        slot[2 * depth + g] = packed


def pack_kernel(bands, *refs):
    sources, targets = refs[:5], refs[5 : bands + 6]
    scratch, outs, sems = refs[bands + 6 : bands + 11], refs[bands + 11 : 2 * bands + 12], refs[2 * bands + 12]
    slots = outs[: bands - 1]
    copies = [pltpu.make_async_copy(a, b, sems.at[n]) for n, (a, b) in enumerate(zip(sources, scratch))]
    for copy in copies:
        copy.start()
    air_ref, level_ref, fuel_ref, class_ref, ignite_ref = scratch
    base = air_tiles(air_ref.shape[1])
    rows, width = level_ref.shape
    sent = []

    def send(n, first=None, count=None):
        source, target = outs[n], targets[n]
        if count is not None:
            source, target = source.at[pl.ds(first, count)], target.at[pl.ds(first, count)]
        sent.append(pltpu.make_async_copy(source, target, sems.at[5 + len(sent)]))
        sent[-1].start()

    copies[0].wait()
    for k in range(1, bands):
        pack_slot(bands, k, air_ref, slots[k - 1])
        send(k - 1, 0, base)
    weights = refs[2 * bands + 13]
    weights[...] = level_weights(1.0, 1.0)
    depth = air_ref.shape[1]
    sub = iota((8, LANES), 0)
    for j in range(width // LANES):
        share = [jnp.zeros((8, LANES), jnp.float32)] * 2
        if j < air_ref.shape[3] // LANES:
            for l in range(depth):
                weight = weights[pl.ds(band_index() * depth + l, 1)]
                for f in range(2):
                    share[f] = share[f] + weight * air_ref[2 + f, l, :, j * LANES : (j + 1) * LANES]
        outs[bands - 1][j, HALO_ROWS:] = jnp.where(sub < 4, share[0], roll(share[1], 4, 0))
        outs[bands][j, HALO_ROWS:] = jnp.where(sub < 4, roll(share[0], 4, 0), share[1])
    for copy in copies[1:]:
        copy.wait()
    fields = [ref[...] for ref in (level_ref, fuel_ref)]
    fields += [ref[...].astype(jnp.float32) for ref in (class_ref, ignite_ref)]
    for n, above in ((bands - 1, False), (bands, True)):
        for j in range(width // LANES):
            outs[n][j, :HALO_ROWS] = halo_pack([field[:, j * LANES : (j + 1) * LANES] for field in fields], above)
        send(n)
    wide = iota((rows, LANES), 1)
    for pair in range(2):
        first, second = fields[2 * pair], fields[2 * pair + 1]
        at = pl.ds(base + pair * (rows // 8), rows // 8)
        to_next = jnp.where(wide < 64, roll(second[:, width - LANES :], 64, 1), first[:, width - LANES :])
        slots[0][at] = to_next.reshape(rows // 8, 8, LANES)
        to_prev = jnp.where(wide < 64, first[:, :LANES], roll(second[:, :LANES], 64, 1))
        slots[bands - 2][at] = to_prev.reshape(rows // 8, 8, LANES)
    send(0, base, 2 * (rows // 8))
    send(bands - 2, base, 2 * (rows // 8))
    for copy in sent:
        copy.wait()


def keep_kernel(bands, air_ref, slot):
    pack_slot(bands, 0, air_ref, slot)


def corner_tiles(next_ref, prev_ref, base, rows):
    lane = iota((rows, LANES), 1)
    result = []
    for pair in range(2):
        at = pl.ds(base + pair * (rows // 8), rows // 8)
        left = prev_ref[at].reshape(rows, LANES)
        right = next_ref[at].reshape(rows, LANES)
        result.append(jnp.where(lane < 64, right, left))
        result.append(roll(jnp.where(lane < 64, left, right), 64, 1))
    return result


def relay_kernel(bands, rows, *refs):
    slots, (up_ref, down_ref, wind_ref, weights) = refs[:bands], refs[bands:]
    tiles = slots[0].shape[0]
    depth = LEVELS // bands
    lane = iota((8, LANES), 1)
    sub = iota((8, LANES), 0)
    for half in range(bands // 2):
        one, two = slots[2 * half], slots[2 * half + 1]

        def body(i, carry, one=one, two=two, half=half):
            first, second = one[i], two[i]
            up_ref[half * tiles + i] = jnp.where(sub < 4, first, roll(second, 4, 0))
            down_ref[half * tiles + i] = jnp.where(sub < 4, roll(first, 4, 0), second)
            return carry

        unrolled(0, tiles, 8, body, 0)

    weights[...] = level_weights(1.0, 1.0)
    inner = [jnp.zeros((8, LANES), jnp.float32)] * 2
    edges = jnp.zeros((8, LANES), jnp.float32)
    level_of = ((lane + 4) & 63) >> 4
    for k in range(bands):
        first = lax.rem(band_index() - k + bands, bands) * depth
        for l in range(depth):
            inner[l % 2] = inner[l % 2] + weights[pl.ds(first + l, 1)] * slots[k][2 * l + 1]
        for g in range(-(-depth // 4)):
            weight = weights[pl.ds(first + 4 * g, 1)]
            for n in range(1, min(4, depth - 4 * g)):
                weight = jnp.where(level_of == n, weights[pl.ds(first + 4 * g + n, 1)], weight)
            edges = edges + weight * slots[k][2 * depth + g]
    inner = inner[0] + inner[1]
    edges = sum(roll(edges, (64 - 8 * (2 * n + 1)) % LANES, 1) for n in range(4))
    wind_ref[0] = jnp.where(lane < 64, inner, edges)
    wind_ref[1] = roll(jnp.where(lane < 64, edges, inner), 64, 1)


def corner_kernel(bands, lane_tiles, up_ref, down_ref, *outs):
    tiles = up_ref.shape[0]
    lane = iota((8, LANES), 1)
    wide = iota((HALO_ROWS, LANES), 1)
    for k in range(bands):
        dest = lax.rem(band_index() + k, bands)
        odd = lax.rem(dest, 2)
        high = (dest + 1) // 2
        right = jnp.minimum(high, lane_tiles - 1)
        left = jnp.maximum(high - 1, 0)
        turn = 64 * odd
        for n, ref in enumerate((up_ref, down_ref)):
            inner, after, before = (ref[j, HALO_ROWS:] for j in (dest // 2, right, left))
            edge = jnp.where(lane < 96 - turn, after, before)
            outs[k][n] = jnp.where(lane < 64, roll(inner, turn, 1), roll(edge, turn, 1))
    at = pl.ds(2, HALO_ROWS // 8)
    up, down = up_ref[tiles - 1, :HALO_ROWS], down_ref[tiles - 1, :HALO_ROWS]
    outs[1][at] = jnp.where(wide < 64, roll(down, 64, 1), up).reshape(HALO_ROWS // 8, 8, LANES)
    up, down = up_ref[0, :HALO_ROWS], down_ref[0, :HALO_ROWS]
    outs[bands - 1][at] = jnp.where(wide < 64, up, roll(down, 64, 1)).reshape(HALO_ROWS // 8, 8, LANES)


def table_vectors(tables_ref):
    lane = iota((8, LANES), 1)
    vectors = []
    for n in range(4):
        vector = jnp.zeros((8, LANES), jnp.float32)
        for category in range(NFUEL):
            vector = jnp.where(lane == category, tables_ref[n, category], vector)
        vectors.append(vector)
    vectors[1] = -1.0 / jnp.where(lane < NFUEL, vectors[1], 1.0)
    return vectors


def pick(vector, index):
    return jnp.take_along_axis(vector, index, axis=1, mode="promise_in_bounds")


def survey_kernel(tables_ref, class_ref, up_ref, down_ref, *outs):
    vectors = table_vectors(tables_ref)
    rows, width = class_ref.shape
    tiles = width // LANES

    def put(j, at, classes):
        index = classes.astype(jnp.int32)
        for vector, out in zip(vectors, outs):
            out[j, at] = pick(vector, index)

    for j in range(tiles):
        for first, ref, above in ((0, up_ref, True), (EDGE + rows, down_ref, False)):
            classes = halo_unpack(ref[j], 2, above)
            for n in range(0, EDGE, 8):
                put(j, slice(first + n, first + n + 8), classes[n : n + 8])

    def body(t, carry):
        for j in range(tiles):
            at = pl.ds(pl.multiple_of(EDGE + 8 * t, 8), 8)
            put(j, at, class_ref[pl.ds(pl.multiple_of(8 * t, 8), 8), j * LANES : (j + 1) * LANES])
        return carry

    unrolled(0, rows // 8, 5, body, 0)


def slab_masks(bands):
    tile, band, tile_count = lax.axis_index("tile"), band_index(), lax.axis_size("tile")
    first_tile, final_tile = tile == 0, tile == tile_count - 1
    first_band, final_band = band == 0, band == bands - 1
    lane, sub = iota((8, LANES), 1), iota((8, LANES), 0)
    low_row = jnp.where(final_tile, 0, 4)
    high_row = jnp.where(first_tile, 8, 4)
    low_lane = jnp.where(final_band, 64, 68)
    high_lane = jnp.where(first_band, 128, 124)
    inside_own = (lane < low_lane) | (lane >= high_lane)
    inside = (inside_own, inside_own & ((sub < low_row) | (sub >= high_row)))
    return first_tile, final_tile, first_band, final_band, inside


def swap(a, b):
    sub = iota((8, LANES), 0)
    a, b = roll(a, 4, 0), roll(b, 4, 0)
    return jnp.where(sub < 4, a, b), jnp.where(sub < 4, b, a)


def strip(t, base=PAD):
    return pl.ds(pl.multiple_of(base + 8 * t, 8), 8)


def fire_steps(bands, tables_ref, tiles, rows, ignite, values_in, values_side, scratch):
    pace, burnt, wind_u, wind_v, energy, vapour = scratch
    first_tile, final_tile, first_band, final_band, inside = slab_masks(bands)
    own = PAD + EDGE
    span = rows + 2 * EDGE
    lane = iota((8, LANES), 1)
    for held in (energy, vapour):
        for j in range(tiles + 1):
            held[j, :16] = jnp.zeros((16, LANES), jnp.float32)
            held[j, span - 16 :] = jnp.zeros((16, LANES), jnp.float32)

    def value_at(n, j, t):
        return values_in[n][j, strip(t, 0)] if j < tiles else values_side[n][strip(t, 0)]

    def kindled(values, t, c):
        return [
            jnp.where(ignite[j, strip(t)] <= c, jnp.minimum(value, -1.0), value) for j, value in enumerate(values)
        ]

    mend_low = first_band & (lane == LANES - 1)
    mend_high = final_band & (lane == 0)

    def mend_lanes(values):
        halo = jnp.where(mend_low, roll(values[0], LANES - 1, 1), values[tiles])
        halo = jnp.where(mend_high, roll(values[tiles - 1], 1, 1), halo)
        return values[:tiles] + [halo]

    def mend_rows(held):
        @pl.when(first_tile)
        def _():
            for j in range(tiles + 1):
                held[j, own - 1 : own] = held[j, own : own + 1]

        @pl.when(final_tile)
        def _():
            for j in range(tiles + 1):
                held[j, own + rows : own + rows + 1] = held[j, own + rows - 1 : own + rows]

    def covers(shape, cell_dim):
        cell, column = iota(shape, cell_dim), iota(shape, 1 - cell_dim)
        start = jnp.where(
            column < 64 + HALO,
            REFINE * column,
            jnp.where(column >= LANES - HALO, REFINE * column + (tiles + 1 - REFINE) * LANES, -LANES * 1000),
        )
        return jnp.where((cell >= start) & (cell < start + REFINE), 1.0, 0.0).astype(jnp.bfloat16)

    cells = (tiles + 1) * LANES
    to_cells = jnp.concatenate([covers((LANES, cells), 1)] * 2, axis=0)
    to_columns = jnp.concatenate([covers((cells, LANES), 0)] * 2, axis=0)

    def parts(value, axis):
        high = value.astype(jnp.bfloat16)
        low = (value - high.astype(jnp.float32)).astype(jnp.bfloat16)
        return jnp.concatenate([high, low], axis=axis)

    def dot(a, b):
        return jnp.dot(a, b, preferred_element_type=jnp.float32)

    def couple(c, wind, chain, fuel_from, fuel_to):
        reach = EDGE - REFINE * (c + 1)
        fire_step = tables_ref[4, c]

        def strips(margin):
            return (EDGE - margin) // 8, -(-(EDGE + rows + margin) // 8)

        coarse = [half for n in range(2) for half in swap(wind[2 * n + 1], wind[2 * n])]
        wide = dot(parts(jnp.concatenate(coarse, axis=0) * wind_gain, 1), to_cells)
        for n, held in enumerate((wind_u, wind_v)):
            for j in range(tiles + 1):
                for half in range(2):
                    value = wide[16 * n + 8 * half : 16 * n + 8 * half + 8, j * LANES : (j + 1) * LANES]
                    for row in range(REFINE):
                        held[j, pl.ds(half * (span // 2) + row, 8, stride=REFINE)] = value

        for s in range(SUBSTEPS):
            before, after = chain[s], chain[s + 1]

            def advance(t, carry, c=c, s=s, fire_step=fire_step, before=before, after=after):
                row = pl.multiple_of(PAD + 8 * t, 8)
                at, flat = strip(t), strip(t, 0)
                centre = [before[j, at] for j in range(tiles + 1)]
                lower = [roll(value, 1, 1) for value in centre]
                upper = [roll(value, LANES - 1, 1) for value in centre]
                result = []
                for j in range(tiles + 1):
                    west = before[j, pl.ds(row - 1, 8)]
                    east = before[j, pl.ds(row + 1, 8)]
                    south = jnp.where(lane == 0, lower[j - 1], lower[j])
                    north = jnp.where(lane == LANES - 1, upper[(j + 1) % (tiles + 1)], upper[j])
                    here = centre[j]
                    back, ahead = here - west, east - here
                    below, above = here - south, north - here
                    a, b = jnp.maximum(back, 0.0), jnp.minimum(ahead, 0.0)
                    d, e = jnp.maximum(below, 0.0), jnp.minimum(above, 0.0)
                    square = (a * a + b * b) + (d * d + e * e)
                    steep = square * lax.rsqrt(jnp.maximum(square, 1.2e-38))
                    gx, gy = back + ahead, below + above
                    blow_u, blow_v = wind_u[j, flat], wind_v[j, flat]
                    if s == 0:
                        speed = fire_step * value_at(0, j, t)
                        pace[j, flat] = speed
                        blow_u, blow_v = blow_u * speed, blow_v * speed
                        wind_u[j, flat] = blow_u
                        wind_v[j, flat] = blow_v
                    else:
                        speed = pace[j, flat]
                    tail = (blow_u * gx + blow_v * gy) * lax.rsqrt((gx * gx + 4.0) + gy * gy)
                    result.append(here - (speed + jnp.maximum(tail, 0.0)) * steep)
                for j in range(tiles + 1):
                    unburnt = jnp.clip(result[j], -0.5, 0.5)
                    if s > 0:
                        unburnt = unburnt + burnt[j, flat]
                    if s < SUBSTEPS - 1:
                        burnt[j, flat] = unburnt
                    else:
                        held = fuel_from[j, at]
                        remain = held * jnp.exp((0.5 * SUBSTEPS - unburnt) * (fire_step * value_at(1, j, t)))
                        spent = held - remain
                        fuel_to[j, at] = remain
                        energy[j, flat] = spent * value_at(2, j, t)
                        vapour[j, flat] = spent * value_at(3, j, t)
                if s == SUBSTEPS - 1 and c < STEPS - 1:
                    result = kindled(result, t, c + 1)
                for j, value in enumerate(mend_lanes(result)):
                    after[j, at] = value
                return carry

            unrolled(*strips(reach + SUBSTEPS - 1 - s), UNROLL_FIRE, advance, 0)
            mend_rows(after)

        totals = []
        for held in (energy, vapour):
            for half in range(2):
                total = []
                for j in range(tiles + 1):
                    value = [held[j, pl.ds(half * (span // 2) + row, 8, stride=REFINE)] for row in range(REFINE)]
                    while len(value) > 1:
                        value = [sum(value[n : n + 2]) for n in range(0, len(value), 2)]
                    total.append(value[0])
                totals.append(jnp.concatenate(total, axis=1))
        flux = dot(parts(jnp.concatenate(totals, axis=0), 1), to_columns)
        forcing = []
        for n, gain in enumerate((heat_gain, vapour_lift * vapour_gain)):
            first, second = (flux[16 * n + 8 * half : 16 * n + 8 * half + 8] for half in range(2))
            halo, inner = swap(second, first)
            scale = air_delta * gain / (REFINE * REFINE)
            forcing.append([jnp.where(mask, value * scale, 0.0) for mask, value in zip(inside, (inner, halo))])
        return forcing

    return couple, kindled, mend_lanes, mend_rows


def first_kernel(bands, tables_ref, level_in, fuel_in, ignite_in, next_ref, prev_ref, wind_own, *refs):
    fire_up, fire_down = refs[:2]
    sides, refs = refs[2 : bands + 2], refs[bands + 2 :]
    values_in = refs[:4]
    level_out, fuel, ignite, flux_out = refs[4:8]
    values_side = refs[8:12]
    lev_a, lev_b = refs[12:14]
    scratch = refs[14:]
    rows, width = level_in.shape
    tiles = width // LANES
    own = PAD + EDGE
    span = rows + 2 * EDGE
    sub = iota((8, LANES), 0)

    corners = corner_tiles(next_ref, prev_ref, air_tiles(LEVELS // bands), rows)
    at = pl.ds(2, HALO_ROWS // 8)
    left, right = (ref[at].reshape(HALO_ROWS, LANES) for ref in (sides[1], sides[bands - 1]))
    wide = iota((HALO_ROWS, LANES), 1)
    upper_side = jnp.where(wide < 64, right, left)
    lower_side = roll(jnp.where(wide < 64, left, right), 64, 1)
    for a, (source, held) in enumerate(((level_in, lev_a), (fuel_in, fuel), (None, None), (ignite_in, ignite))):
        upper, lower = halo_unpack(upper_side, a, True), halo_unpack(lower_side, a, False)
        if held is None:
            side = jnp.concatenate([upper, corners[a], lower], axis=0).astype(jnp.int32)
            vectors = table_vectors(tables_ref)
            for n in range(span // 8):
                for vector, out in zip(vectors, values_side):
                    out[8 * n : 8 * n + 8] = pick(vector, side[8 * n : 8 * n + 8])
            continue
        for j in range(tiles):
            held[j, PAD:own] = halo_unpack(fire_up[j], a, True)
            held[j, own : own + rows] = source[:, j * LANES : (j + 1) * LANES].astype(jnp.float32)
            held[j, own + rows : own + rows + EDGE] = halo_unpack(fire_down[j], a, False)
        held[tiles, PAD:own] = upper
        held[tiles, own : own + rows] = corners[a]
        held[tiles, own + rows : own + rows + EDGE] = lower
    spare = jnp.zeros((tiles + 1, PAD, LANES), jnp.float32)
    for held in (lev_a, lev_b):
        held[:, :PAD] = spare
        held[:, PAD + span :] = spare

    couple, kindled, mend_lanes, mend_rows = fire_steps(
        bands, tables_ref, tiles, rows, ignite, values_in, values_side, scratch
    )

    def kindle(t, carry):
        values = mend_lanes(kindled([lev_a[j, strip(t)] for j in range(tiles + 1)], t, 0))
        for j, value in enumerate(values):
            lev_a[j, strip(t)] = value
        return carry

    unrolled(0, span // 8, UNROLL_LOOKUP, kindle, 0)
    mend_rows(lev_a)


    inside = slab_masks(bands)[4]
    above, below = (sum(ref[n] for ref in sides) for n in range(2))
    halo_u = jnp.where(sub < 4, below, roll(above, 4, 0))
    halo_v = jnp.where(sub < 4, roll(below, 4, 0), above)
    wind = []
    for value, halo in ((wind_own[0], halo_u), (wind_own[1], halo_v)):
        wind += [jnp.where(inside[0], value, 0.0), jnp.where(inside[1], halo, 0.0)]
    forcing = couple(0, wind, (lev_a, lev_b, lev_a, lev_b, level_out), fuel, fuel)
    for n in range(2):
        for part in range(2):
            flux_out[2 * n + part] = forcing[n][part]


def main_kernel(bands, tables_ref, level_in, fuel_in, ignite, flux_in, *refs):
    slots = refs[:bands]
    edge_up, edge_down = refs[bands : bands + 2]
    values_in = refs[bands + 2 : bands + 6]
    values_side = refs[bands + 6 : bands + 10]
    level_out, fuel_out = refs[bands + 10 : bands + 12]
    outs = refs[bands + 12 : 2 * bands + 12]
    scratch = refs[2 * bands + 12 :]
    lev_a, lev_b, fuel = scratch[:3]
    air_a, air_b, weights = scratch[9:12]
    rows, width = level_out.shape
    tiles = width // LANES
    depth = LEVELS // bands
    count = air_tiles(depth)
    own = PAD + EDGE
    lane = iota((8, LANES), 1)
    band = band_index()
    couple = fire_steps(bands, tables_ref, tiles, rows, ignite, values_in, values_side, scratch[3:9])[0]

    sub = iota((8, LANES), 0)
    inside = slab_masks(bands)[4]

    def layer_at(k, part, shift=0):
        return pl.ds(pl.multiple_of((k + 1) * 24 + 8 * part, 8) + shift, 8)

    def put(held, f, k, part, value):
        held[f, layer_at(k, part)] = value
        if part == 2:
            held[f, layer_at(k, 0)] = value

    for k in range(bands):
        source = lax.rem(band - k + bands, bands)
        half = k // 2

        def whole(i, k=k, half=half):
            below, above = edge_down[half * count + i], edge_up[half * count + i]
            if k % 2 == 0:
                halo = jnp.where(sub < 4, below, roll(above, 4, 0))
            else:
                halo = jnp.where(sub < 4, roll(below, 4, 0), above)
            return slots[k][i], halo

        for g in range(-(-depth // 4)):
            edges = whole(2 * depth + g)
            for l in range(4 * g, min(4 * g + 4, depth)):
                for p in range(2):
                    both = whole(2 * l + p)
                    for part in range(2):
                        edge = roll(edges[part], (64 - 8 * ((l - 4 * g) * 2 + p)) % LANES, 1)
                        values = (
                            jnp.where(lane < 64, both[part], edge),
                            roll(jnp.where(lane < 64, edge, both[part]), 64, 1),
                        )
                        for f in range(2):
                            value = values[f] * vapour_lift if 2 * p + f == 1 else values[f]
                            value = jnp.where(inside[part], value, 0.0)
                            put(air_a, 2 * p + f, source * depth + l, part + 1, value)
    nothing = jnp.zeros((8, LANES), jnp.float32)
    for held in (air_a, air_b):
        for f in range(4):
            for part in range(3):
                held[f, layer_at(-1, part)] = nothing
                held[f, layer_at(LEVELS, part)] = nothing

    weights[0] = level_weights(2.0, float(LEVELS))
    weights[1] = level_weights(1.0, 1.0)
    def blow(total, k, result):
        weight = weights[1, pl.ds(k, 1)]
        return [a + weight * b for a, b in zip(total, result)]

    calm = [nothing] * 4
    spread = air_delta * diffusion
    mixing = [jnp.where(mask, spread, 0.0) for mask in inside]
    lifting = [jnp.where(mask, 0.5 * lift_gain * air_delta, 0.0) for mask in inside]
    state, other = air_a, air_b
    for c in range(STEPS):
        if c == 0:
            forcing = [[flux_in[2 * n + part] for part in range(2)] for n in range(2)]
        else:
            chain = (level_in if c == 1 else lev_a, lev_b, lev_a, lev_b, lev_a)
            forcing = couple(c, wind, chain, fuel_in if c == 1 else fuel, fuel)

        def air_step(k, part, height, state=state, forcing=forcing):
            at = layer_at(k, part + 1)
            here = [state[f, at] for f in range(4)]
            west = [state[f, layer_at(k, part + 1, -1)] for f in range(4)]
            east = [state[f, layer_at(k, 1 if part == 0 else 0, 1)] for f in range(4)]
            south = [roll(value, 1, 1) for value in here]
            north = [roll(value, LANES - 1, 1) for value in here]
            u, v = air_delta * here[2], air_delta * here[3]
            mix = mixing[part]
            to_west, to_east = mix + jnp.maximum(u, 0.0), mix - jnp.minimum(u, 0.0)
            to_south, to_north = mix + jnp.maximum(v, 0.0), mix - jnp.minimum(v, 0.0)
            keep = (1.0 - 6.0 * spread) - (jnp.abs(u) + jnp.abs(v))
            result = []
            for f in range(4):
                new = keep * here[f] + mix * (state[f, layer_at(k - 1, part + 1)] + state[f, layer_at(k + 1, part + 1)])
                new = new + (to_west * west[f] + to_east * east[f]) + (to_south * south[f] + to_north * north[f])
                if f < 2:
                    new = new + height * forcing[f][part]
                else:
                    low, high = (west, east) if f == 2 else (south, north)
                    new = new + lifting[part] * ((high[0] - low[0]) + (high[1] - low[1]))
                result.append(new)
            return result

        if c < STEPS - 1:

            def layer(k, carry, other=other, air_step=air_step):
                height = weights[0, pl.ds(k, 1)]
                result = [air_step(k, part, height) for part in range(2)]
                for part in range(2):
                    for f in range(4):
                        put(other, f, k, part + 1, result[part][f])
                return blow(carry, k, [result[part][f] for f in (2, 3) for part in range(2)])

            wind = unrolled(0, LEVELS, UNROLL_AIR, layer, calm)
            state, other = other, state
        else:
            for k in range(bands):
                first = lax.rem(band + k, bands) * depth

                def final(l, carry, out=outs[k], first=first, air_step=air_step):
                    result = air_step(first + l, 0, weights[0, pl.ds(first + l, 1)])
                    result[1] = result[1] * (1.0 / vapour_lift)
                    for p in range(2):
                        out[2 * l + p] = jnp.where(lane < 64, result[2 * p], roll(result[2 * p + 1], 64, 1))
                    return carry

                unrolled(0, depth, UNROLL_FINAL, final, 0)

    for j in range(tiles):
        level_out[:, j * LANES : (j + 1) * LANES] = lev_a[j, own : own + rows]
        fuel_out[:, j * LANES : (j + 1) * LANES] = fuel[j, own : own + rows]


def unpack_kernel(bands, shifts, *refs):
    out = refs[-1]
    depth = out.shape[1]
    lane = iota((8, LANES), 1)
    if len(refs) > len(shifts) + 1:
        out[...] = refs[len(shifts)][...]
    for k, held in zip(shifts, refs):
        source = lax.rem(band_index() - k + bands, bands)
        odd = lax.rem(source, 2)
        cols = pl.ds(pl.multiple_of((source // 2) * LANES, LANES), LANES)
        mine = (lane >= 64 * odd) & (lane < 64 * odd + 64)

        is_odd = jnp.full((8, LANES), odd, jnp.int32) == 1

        def body(l, carry, slot=held, is_odd=is_odd, cols=cols, mine=mine):
            for p in range(2):
                both = slot[2 * l + p]
                turned = roll(both, 64, 1)
                for f, value in enumerate((jnp.where(is_odd, turned, both), jnp.where(is_odd, both, turned))):
                    old = out[2 * p + f, l, :, cols]
                    out[2 * p + f, l, :, cols] = jnp.where(mine, value, old)
            return carry

        unrolled(0, depth, 10, body, 0)


def shape(*dims):
    return jax.ShapeDtypeStruct(dims, jnp.float32)


def vmem():
    return pl.BlockSpec(memory_space=pltpu.VMEM)


def smem():
    return pl.BlockSpec(memory_space=pltpu.SMEM)


def local(
    air_state,
    fire_level,
    fuel_left,
    fuel_class,
    ignition,
    plan,
    spread_rate,
    burn_time,
    heat_content,
    moisture_content,
):
    steps = jnp.pad(plan.astype(jnp.float32) * fire_delta, (0, NFUEL - STEPS))
    tables = jnp.stack([spread_rate, burn_time, heat_content, moisture_content, steps])
    bands = lax.axis_size(BANDS)
    tile_count = lax.axis_size("tile")
    depth = air_state.shape[1]
    rows, width = fire_level.shape
    tiles = width // LANES
    count = air_tiles(depth)
    extra = 2 * (rows // 8)
    params = pltpu.CompilerParams(vmem_limit_bytes=VMEM_LIMIT)

    sizes = [count + (extra if k in (1, bands - 1) else 0) for k in range(bands)]
    packed = pl.pallas_call(
        functools.partial(pack_kernel, bands),
        out_shape=[shape(size, 8, LANES) for size in sizes[1:]] + [shape(tiles, SENT_ROWS, LANES)] * 2,
        in_specs=[pl.BlockSpec(memory_space=pltpu.HBM)] * 5,
        out_specs=[pl.BlockSpec(memory_space=pltpu.HBM)] * (bands + 1),
        scratch_shapes=[
            pltpu.VMEM(x.shape, x.dtype) for x in (air_state, fire_level, fuel_left, fuel_class, ignition)
        ]
        + [pltpu.VMEM((size, 8, LANES), jnp.float32) for size in sizes[1:]]
        + [pltpu.VMEM((tiles, SENT_ROWS, LANES), jnp.float32)] * 2
        + [pltpu.SemaphoreType.DMA((bands + 8,)), pltpu.VMEM((LEVELS, LANES), jnp.float32)],
        compiler_params=pltpu.CompilerParams(vmem_limit_bytes=PACK_LIMIT),
        name="pack",
    )(air_state, fire_level, fuel_left, fuel_class, ignition)
    slots, up, down = packed[: bands - 1], packed[bands - 1], packed[bands]
    kept = pl.pallas_call(
        functools.partial(keep_kernel, bands),
        out_shape=shape(count, 8, LANES),
        in_specs=[vmem()],
        out_specs=vmem(),
        compiler_params=params,
        cost_estimate=pl.CostEstimate(flops=KEEP_FLOPS, bytes_accessed=0, transcendentals=0),
        name="keep",
    )(air_state)

    rise = [(i, i + 1) for i in range(tile_count - 1)]
    sink = [(j, i) for i, j in rise]

    def turn(values):
        moved = [values[0]]
        for k in range(1, bands):
            moved.append(lax.ppermute(values[k], BANDS, [(i, (i + k) % bands) for i in range(bands)]))
        return moved

    fire_up = lax.ppermute(down, "tile", rise)
    fire_down = lax.ppermute(up, "tile", sink)
    slots = turn([kept, *slots])
    edges = (bands // 2) * count
    up, down, wind = pl.pallas_call(
        functools.partial(relay_kernel, bands, rows),
        out_shape=[shape(edges, 8, LANES)] * 2 + [shape(2, 8, LANES)],
        in_specs=[vmem()] * bands,
        out_specs=[vmem()] * 3,
        scratch_shapes=[pltpu.VMEM((LEVELS, LANES), jnp.float32)],
        compiler_params=params,
        cost_estimate=pl.CostEstimate(flops=RELAY_FLOPS, bytes_accessed=0, transcendentals=0),
        name="relay",
    )(*slots)
    edge_up = lax.ppermute(down, "tile", rise)
    edge_down = lax.ppermute(up, "tile", sink)
    sides = pl.pallas_call(
        functools.partial(corner_kernel, bands, air_state.shape[3] // LANES),
        out_shape=[
            shape(2 + (HALO_ROWS // 8 if k in (1, bands - 1) else 0), 8, LANES) for k in range(bands)
        ],
        in_specs=[vmem()] * 2,
        out_specs=[vmem()] * bands,
        compiler_params=params,
        name="corners",
    )(fire_up, fire_down)
    sides = turn(sides)

    span = rows + 2 * EDGE
    values = pl.pallas_call(
        survey_kernel,
        out_shape=[shape(tiles, span, LANES)] * 4,
        in_specs=[smem()] + [vmem()] * 3,
        out_specs=[vmem()] * 4,
        compiler_params=params,
        cost_estimate=pl.CostEstimate(flops=SURVEY_FLOPS, bytes_accessed=0, transcendentals=0),
        name="survey",
    )(tables, fuel_class, fire_up, fire_down)
    padded = (tiles + 1, span + 2 * PAD, LANES)
    fire = pltpu.VMEM(padded, jnp.float32)
    flat = pltpu.VMEM((tiles + 1, span, LANES), jnp.float32)
    atmosphere = pltpu.VMEM((4, (LEVELS + 2) * 24, LANES), jnp.float32)
    level, fuel, ignite, flux, *values_side = pl.pallas_call(
        functools.partial(first_kernel, bands),
        out_shape=[shape(*padded)] * 3 + [shape(4, 8, LANES)] + [shape(span, LANES)] * 4,
        in_specs=[smem()] + [vmem()] * (12 + bands),
        out_specs=[vmem()] * 8,
        scratch_shapes=[fire] * 2 + [flat] * 6,
        compiler_params=params,
        cost_estimate=pl.CostEstimate(flops=FIRST_FLOPS, bytes_accessed=0, transcendentals=0),
        name="first",
    )(
        tables,
        fire_level,
        fuel_left,
        ignition,
        slots[bands - 1],
        slots[1],
        wind,
        fire_up,
        fire_down,
        *sides,
        *values,
    )
    results = pl.pallas_call(
        functools.partial(main_kernel, bands),
        out_shape=[shape(rows, width)] * 2 + [shape(2 * depth, 8, LANES)] * bands,
        in_specs=[smem()] + [vmem()] * (4 + bands + 10),
        out_specs=[vmem()] * (2 + bands),
        scratch_shapes=[fire] * 3 + [flat] * 6 + [atmosphere] * 2 + [pltpu.VMEM((2, LEVELS, LANES), jnp.float32)],
        compiler_params=params,
        name="window",
    )(
        tables,
        level,
        fuel,
        ignite,
        flux,
        *slots,
        edge_up,
        edge_down,
        *values,
        *values_side,
    )
    level_out, fuel_out = results[:2]
    slabs = turn(results[2:])
    air_out = []
    for shifts in (range(2), range(2, bands)):
        air_out = [
            pl.pallas_call(
                functools.partial(unpack_kernel, bands, shifts),
                out_shape=shape(*air_state.shape),
                in_specs=[vmem()] * (len(shifts) + len(air_out)),
                out_specs=vmem(),
                compiler_params=params,
                cost_estimate=pl.CostEstimate(flops=UNPACK_FLOPS, bytes_accessed=0, transcendentals=0),
                name=f"unpack_{shifts[0]}",
            )(*(slabs[k] for k in shifts), *air_out)
        ]
    air_out = air_out[0]
    return (air_out, level_out, fuel_out)


def solution(mesh):
    placed = (
        P(None, ("sect", "sub"), ("group", "tile"), None),
        P(("group", "tile"), ("sect", "sub")),
        P(("group", "tile"), ("sect", "sub")),
        P(("group", "tile"), ("sect", "sub")),
        P(("group", "tile"), ("sect", "sub")),
        P(),
        P(),
        P(),
        P(),
        P(),
    )
    return jax.shard_map(
        local,
        mesh=mesh,
        in_specs=placed,
        out_specs=(
            P(None, ("sect", "sub"), ("group", "tile"), None),
            P(("group", "tile"), ("sect", "sub")),
            P(("group", "tile"), ("sect", "sub")),
        ),
        check_vma=False,
    )
```
